32 devices in a mesh: ctx: 16 (over z, y, core), mp: 2 (over x).
Axes of the slice: x: 2, y: 2, z: 4, core: 2. Of those that a mesh axis runs over, the one named last changes fastest.
Arguments:
- queries: bfloat16 [8192, 4096], P('ctx', 'mp'), may hold values from -15 to 15
- keys: bfloat16 [8192, 2048], P('ctx', 'mp'), may hold values from -15 to 15
- values: bfloat16 [8192, 2048], P('ctx', 'mp'), may hold values from -6 to 6
- grad_out: bfloat16 [8192, 4096], P(('ctx', 'mp')), may hold values from -6 to 6
- band_mask: int32 [64, 9], replicated, may hold values from 0 to 1, as said below
- segment_ids: int32 [8192], replicated, may hold values from 0 to 7, never falling along the last dimension, each value on 1 to 4096 neighbouring positions
Outputs:
- attn_out: bfloat16 [8192, 4096], P(('ctx', 'mp'))
- grad_queries: bfloat16 [8192, 4096], P('ctx', 'mp')
- grad_keys: bfloat16 [8192, 2048], P('ctx', 'mp')
- grad_values: bfloat16 [8192, 2048], P('ctx', 'mp')
The draws below stay inside these ranges and needn't reach their ends.
Inputs may be any that keep to these rules, and one draw needn't show every extreme that they name: band_mask[b, o] is 1 when query block b may see the key block o blocks before it; offset 0 is always 1. `segment_ids`: segment numbers never fall along the sequence.
All inputs are finite; a program needn't handle non-finite values.
Results may differ from the reference program's by a relative error of at most 0.03.
Values may be sent and summed in bfloat16 or wider, within the bound.
No kernel may reach another device: no remote copies, remote signals or barrier semaphores. Data moves between devices by JAX's collectives and lax.ppermute only.
A program may use at most 128 MiB of HBM per device.

```python
import math
import jax
import jax.numpy as jnp
import numpy as np
from jax import lax

Q_HEADS = 32
KV_HEADS = 16
HEAD = 128
WINDOW = 1024
BLOCK = 128
TOKENS = 8192
NBAND = 9
NQB = 64
SEG_COUNT = 8
SEG_MOST = 4096


def paired_fields(key):
    query_base = jax.random.normal(jax.random.fold_in(key, 11), (TOKENS, Q_HEADS, HEAD), jnp.float32)
    key_base = jax.random.normal(jax.random.fold_in(key, 12), (TOKENS, KV_HEADS, HEAD), jnp.float32)
    query_base = jnp.clip(query_base, -15.0, 15.0)
    key_base = jnp.clip(key_base, -15.0, 15.0)
    return (query_base.reshape(TOKENS, Q_HEADS * HEAD), key_base.reshape(TOKENS, KV_HEADS * HEAD))


def draw_queries(key, part):
    return paired_fields(key)[0].astype(jnp.bfloat16)


def draw_keys(key, part):
    return paired_fields(key)[1].astype(jnp.bfloat16)


def draw_band_mask(key, part):
    bits = (jax.random.randint(key, (NQB, NBAND), 0, 10) < 7).astype(jnp.int32)
    return bits.at[:, 0].set(1)


def block_levels(stream_key, dims, pieces, smallest, largest):
    level, own = 1.0, jax.random.fold_in(stream_key, 6)
    for axis_at, parts in pieces:
        steps = jnp.exp(jax.random.uniform(jax.random.fold_in(own, axis_at), (parts,), jnp.float32, smallest / len(pieces), largest / len(pieces)))
        level = level * jnp.repeat(steps, dims[axis_at] // parts).reshape([-1 if axis == axis_at else 1 for axis in range(len(dims))])
    return level


def profile(number_of, total, limit, skew):
    portions = [(1 << 20) // math.isqrt(standing ** skew) + 1 for standing in range(2, number_of + 1)]
    surplus, given = total - limit - (number_of - 1), [1] * (number_of - 1)
    while surplus > 0:
        movable = [i for i in range(number_of - 1) if given[i] < limit]
        whole, budget = sum([portions[i] for i in movable]), surplus
        for i in movable:
            more = min(limit - given[i], max(1, budget * portions[i] // whole), surplus)
            given[i] = given[i] + more
            surplus = surplus - more
    return np.array([limit] + given)


def uneven_parts(stream_key, number_of, total, most, slope):
    if number_of == 2:
        one = jax.random.randint(stream_key, (), max(1, total - most), min(most, total - 1) + 1)
        return jnp.stack([one, total - one])
    sizes = jnp.asarray(profile(number_of, total, most, slope), jnp.int32)
    couples = (number_of - 1) // 2
    donor, receiver = sizes[1:1 + 2 * couples:2], sizes[2:2 + 2 * couples:2]
    room = jnp.minimum(donor - 1, most - receiver)
    passed = jax.random.randint(jax.random.fold_in(stream_key, 1), (couples,), 0, 1 << 20) % (room + 1)
    sizes = sizes.at[1:1 + 2 * couples:2].set(donor - passed).at[2:2 + 2 * couples:2].set(receiver + passed)
    return sizes[jax.random.permutation(jax.random.fold_in(stream_key, 2), number_of)]


def normal_values(key, extent, spread, most, shards=(), held_as=jnp.bfloat16):
    loudness = block_levels(key, extent, shards, -0.22, 0.18) if shards else 1.0
    result = jax.random.normal(key, extent, jnp.float32) * spread * loudness
    return jnp.minimum(jnp.maximum(result, -most), most).astype(held_as)


def setup_inputs(seed: int = 0) -> dict:
    seeds = jax.random.split(jax.random.key(seed), 7)
    queries = draw_queries(jax.random.fold_in(seeds[6], 71), 0)
    keys = draw_keys(jax.random.fold_in(seeds[6], 71), 0)
    values = normal_values(seeds[2], (TOKENS, KV_HEADS * HEAD), 1.0, 6.0, ((0, 16), (1, 2)))
    grad_out = normal_values(seeds[3], (TOKENS, Q_HEADS * HEAD), 1.0, 6.0, ((0, 32),))
    band_mask = draw_band_mask(jax.random.fold_in(seeds[6], 71), 0)
    segment_ids = jnp.searchsorted(jnp.cumsum(uneven_parts(seeds[5], SEG_COUNT, TOKENS, SEG_MOST, 2)), jnp.arange(TOKENS), side="right").astype(jnp.int32)
    return dict(queries=queries, keys=keys, values=values, grad_out=grad_out, band_mask=band_mask, segment_ids=segment_ids)


ATTN_SCALE = 168.0 ** -0.5
NEG_FILL = -1e30


def block_mask(seg_query, seg_key, band_row):
    rows_query = seg_query.shape[0]
    width_keys = seg_key.shape[0]
    distance = WINDOW + jnp.arange(rows_query)[:, None] - jnp.arange(width_keys)[None, :]
    allowed = jnp.repeat(band_row[::-1], BLOCK)
    return (distance >= 0) & (distance < WINDOW) & (seg_query[:, None] == seg_key[None, :]) & (allowed[None, :] == 1)


def reference(queries, keys, values, grad_out, band_mask, segment_ids):
    q_per_kv = Q_HEADS // KV_HEADS
    span_keys = WINDOW + BLOCK
    block_total = TOKENS // BLOCK
    key_pad = jnp.concatenate([jnp.zeros((WINDOW, KV_HEADS * HEAD), keys.dtype), keys]).reshape(TOKENS + WINDOW, KV_HEADS, HEAD)
    value_pad = jnp.concatenate([jnp.zeros((WINDOW, KV_HEADS * HEAD), values.dtype), values]).reshape(TOKENS + WINDOW, KV_HEADS, HEAD)
    seg_padded = jnp.concatenate([jnp.full((WINDOW,), -1, jnp.int32), segment_ids.astype(jnp.int32)])

    def step(carry, block_idx):
        key_grad, value_grad = carry
        start = (block_idx * BLOCK).astype(jnp.int32)
        query_blk = lax.dynamic_slice_in_dim(queries, start, BLOCK, 0).reshape(BLOCK, KV_HEADS, q_per_kv, HEAD).astype(jnp.float32)
        key_slab = lax.dynamic_slice_in_dim(key_pad, start, span_keys, 0).astype(jnp.float32)
        value_slab = lax.dynamic_slice_in_dim(value_pad, start, span_keys, 0).astype(jnp.float32)
        seg_query = lax.dynamic_slice_in_dim(segment_ids.astype(jnp.int32), start, BLOCK, 0)
        seg_key = lax.dynamic_slice_in_dim(seg_padded, start, span_keys, 0)
        band_row = lax.dynamic_index_in_dim(band_mask, block_idx, 0, keepdims=False)
        valid = block_mask(seg_query, seg_key, band_row)
        scores = jnp.einsum("qkgd,skd->kgqs", query_blk, key_slab) * ATTN_SCALE
        scores = jnp.where(valid, scores, NEG_FILL)
        row_max = jnp.max(scores, axis=-1, keepdims=True)
        log_norm = row_max + jnp.log(jnp.sum(jnp.exp(scores - row_max), axis=-1, keepdims=True))
        prob_bf = jnp.exp(scores - log_norm).astype(jnp.bfloat16)
        prob_wide = prob_bf.astype(jnp.float32)
        attended = jnp.einsum("kgqs,skd->qkgd", prob_wide, value_slab).astype(jnp.bfloat16)
        grad_blk = lax.dynamic_slice_in_dim(grad_out, start, BLOCK, 0).reshape(BLOCK, KV_HEADS, q_per_kv, HEAD).astype(jnp.float32)
        delta = jnp.sum(grad_blk * attended.astype(jnp.float32), axis=-1).transpose(1, 2, 0)[..., None]
        value_part = jnp.einsum("kgqs,qkgd->skd", prob_wide, grad_blk)
        grad_prob = jnp.einsum("qkgd,skd->kgqs", grad_blk, value_slab)
        grad_score = (prob_wide * (grad_prob - delta)).astype(jnp.bfloat16).astype(jnp.float32)
        grad_query = (jnp.einsum("kgqs,skd->qkgd", grad_score, key_slab) * ATTN_SCALE).astype(jnp.bfloat16)
        key_part = jnp.einsum("kgqs,qkgd->skd", grad_score, query_blk) * ATTN_SCALE
        key_grad = lax.dynamic_update_slice_in_dim(key_grad, lax.dynamic_slice_in_dim(key_grad, start, span_keys, 0) + key_part, start, 0)
        value_grad = lax.dynamic_update_slice_in_dim(value_grad, lax.dynamic_slice_in_dim(value_grad, start, span_keys, 0) + value_part, start, 0)
        return (key_grad, value_grad), (attended.reshape(BLOCK, Q_HEADS * HEAD), grad_query.reshape(BLOCK, Q_HEADS * HEAD))

    zeros = jnp.zeros((TOKENS + WINDOW, KV_HEADS, HEAD), jnp.float32)
    (key_grad, value_grad), (attended_all, grad_all) = lax.scan(step, (zeros, zeros), jnp.arange(block_total, dtype=jnp.int32))
    attn_out = attended_all.reshape(TOKENS, Q_HEADS * HEAD)
    grad_queries = grad_all.reshape(TOKENS, Q_HEADS * HEAD)
    grad_keys = key_grad[WINDOW:].reshape(TOKENS, KV_HEADS * HEAD).astype(jnp.bfloat16)
    grad_values = value_grad[WINDOW:].reshape(TOKENS, KV_HEADS * HEAD).astype(jnp.bfloat16)
    return (attn_out, grad_queries, grad_keys, grad_values)
```

```python
import functools
import math

import jax
import jax.numpy as jnp
from jax import lax
from jax.experimental import pallas as pl
from jax.experimental.pallas import tpu as pltpu
from jax.sharding import PartitionSpec as P

KV_HEADS = 16
GROUP = 2
HEAD = 128
WINDOW = 1024
BLOCK = 128
SPAN = WINDOW // BLOCK + 1
CHUNKS = 2
ATTN_SCALE = 168.0 ** (-0.5)
EXP2_SCALE = ATTN_SCALE * math.log2(math.e)
MASKED = -1e30
FAR = 1 << 20
AXES = ("ctx", "mp")
NT = (((1,), (1,)), ((), ()))
NN = (((1,), (0,)), ((), ()))


def dot(a, b, dims=NN):
    return lax.dot_general(a, b, dims, preferred_element_type=jnp.float32)


def routes(target, n_ctx, n_mp):
    out = []
    for c in range(n_ctx):
        for m in range(n_mp):
            d = target(c, m)
            if 0 <= d[0] < n_ctx:
                out.append((c * n_mp + m, d[0] * n_mp + d[1]))
    return out


def copies_kernel(plan, n_in, sc_ref, *refs):
    sem = refs[-1]
    jobs = []
    for src, src_at, dst, dst_at, rows, cols in plan(sc_ref[0], sc_ref[1]):
        jobs.append(
            pltpu.make_async_copy(
                refs[src].at[pl.ds(0, rows), pl.ds(src_at, cols)],
                refs[n_in + dst].at[pl.ds(0, rows), pl.ds(dst_at, cols)],
                sem.at[len(jobs)],
            )
        )
    for job in jobs:
        job.start()
    for job in jobs:
        job.wait()


def run_copies(plan, place, arrays, outs, count):
    hbm = pl.BlockSpec(memory_space=pl.ANY)
    moved = sum(math.prod(o.shape) * o.dtype.itemsize for o in outs)
    return pl.pallas_call(
        functools.partial(copies_kernel, plan, len(arrays)),
        in_specs=[pl.BlockSpec(memory_space=pltpu.SMEM)] + [hbm] * len(arrays),
        out_specs=[hbm] * len(outs),
        out_shape=outs,
        scratch_shapes=[pltpu.SemaphoreType.DMA((count,))],
        cost_estimate=pl.CostEstimate(flops=0, bytes_accessed=2 * moved, transcendentals=0),
    )(place, *arrays)


def attention_kernel(n_mp, rows, sc_ref, open_ref, lo_ref, *refs):
    n_do = 2 * n_mp
    q_own, q_oth, k_own, k_oth, v_own, v_oth, h_same, h_oth = refs[:8]
    do_in = refs[8 : 8 + n_do]
    outs = refs[8 + n_do : 8 + 2 * n_do + 6]
    o_out = outs[:n_do]
    dq_same, dq_oth, dkv_same, dkv_oth, dh_same, dh_oth = outs[n_do:]
    qs, ks, vs, k_t, v_t, dos, os, dqs, dk, dv, s_ref, e_ref = refs[8 + 2 * n_do + 6 :]
    core, mp = sc_ref[0], sc_ref[1]
    piece = rows // n_mp
    same = pl.ds(pl.multiple_of(core * rows, rows), rows)
    oth = pl.ds(pl.multiple_of((1 - core) * rows, rows), rows)
    same_kv = pl.ds(pl.multiple_of(WINDOW + core * rows, rows), rows)
    oth_kv = pl.ds(pl.multiple_of(WINDOW + (1 - core) * rows, rows), rows)

    def piece_at(dk_, dm):
        k_at = core if dk_ == 0 else 1 - core
        return pl.ds(pl.multiple_of(k_at * rows + lax.rem(mp + dm, n_mp) * piece, piece), piece)

    qs[same, :] = q_own[...]
    qs[oth, :] = q_oth[...]
    ks[same, :] = h_same[:, :HEAD]
    ks[oth, :] = h_oth[:, :HEAD]
    ks[same_kv, :] = k_own[...]
    ks[oth_kv, :] = k_oth[...]
    vs[same, :] = h_same[:, HEAD:]
    vs[oth, :] = h_oth[:, HEAD:]
    vs[same_kv, :] = v_own[...]
    vs[oth_kv, :] = v_oth[...]
    for at in range(n_do):
        dos[piece_at(at // n_mp, n_mp - at % n_mp), :] = do_in[at][...]
    dk[...] = jnp.zeros_like(dk)
    dv[...] = jnp.zeros_like(dv)
    for t in range(ks.shape[0] // 256):
        at = slice(t * 256, t * 256 + 256)
        k_t[:, at] = ks[at, :].T
        v_t[:, at] = vs[at, :].T

    row = lax.broadcasted_iota(jnp.int32, (BLOCK, GROUP * BLOCK), 0)
    lane = lax.broadcasted_iota(jnp.int32, (BLOCK, GROUP * BLOCK), 1)
    causal = row <= lax.rem(lane, BLOCK)

    def block(b, carry):
        at_q = pl.ds(pl.multiple_of(b * BLOCK, BLOCK), BLOCK)
        q_blk = jnp.concatenate([qs[at_q, :HEAD], qs[at_q, HEAD:]], axis=0)
        lo = lo_ref[:, at_q]
        lo = jnp.concatenate([lo, lo], axis=1)
        top = jnp.full((8, GROUP * BLOCK), MASKED, jnp.float32)
        for j in range(SPAN):
            k_at = pl.ds(pl.multiple_of((b + j) * BLOCK, BLOCK), BLOCK)
            part = slice(j * BLOCK, j * BLOCK + BLOCK)
            s = dot(ks[k_at, :], q_blk, NT)
            closed = jnp.where(open_ref[b * SPAN + SPAN - 1 - j] == 1, 0, FAR)
            valid = row >= jnp.maximum(lo - (b + j) * BLOCK, closed)
            if j == SPAN - 1:
                valid = valid & causal
            s = jnp.where(valid, s, MASKED)
            s_ref[part, :] = s
            top = jnp.maximum(top, jnp.max(s.reshape(BLOCK // 8, 8, GROUP * BLOCK), axis=0))
        top = jnp.max(top, axis=0, keepdims=True)
        total = jnp.zeros((8, GROUP * BLOCK), jnp.float32)
        for j in range(SPAN):
            part = slice(j * BLOCK, j * BLOCK + BLOCK)
            e = jnp.exp2((s_ref[part, :] - top) * EXP2_SCALE)
            total = total + jnp.sum(e.reshape(BLOCK // 8, 8, GROUP * BLOCK), axis=0)
            e_ref[part, :] = e.astype(jnp.bfloat16)
        inverse = 1.0 / jnp.sum(total, axis=0, keepdims=True)
        at_keys = pl.ds(pl.multiple_of(b * BLOCK, BLOCK), SPAN * BLOCK)
        o_t = (dot(v_t[:, at_keys], e_ref[...]) * inverse).astype(jnp.bfloat16)
        os[at_q, :HEAD] = o_t[:, :BLOCK].T
        os[at_q, HEAD:] = o_t[:, BLOCK:].T
        do_t = jnp.concatenate([dos[at_q, :HEAD].T, dos[at_q, HEAD:].T], axis=1)
        do_t = (do_t.astype(jnp.float32) * inverse).astype(jnp.bfloat16)
        delta = jnp.sum(
            do_t.astype(jnp.float32) * o_t.astype(jnp.float32), axis=0, keepdims=True
        )
        dq_t = jnp.zeros((HEAD, GROUP * BLOCK), jnp.float32)
        for j in range(SPAN):
            k_at = pl.ds(pl.multiple_of((b + j) * BLOCK, BLOCK), BLOCK)
            part = slice(j * BLOCK, j * BLOCK + BLOCK)
            dp = dot(vs[k_at, :], do_t)
            e = e_ref[part, :]
            ds = (e.astype(jnp.float32) * (dp - delta)).astype(jnp.bfloat16)
            dv[k_at, :] += dot(e, do_t, NT)
            dk[k_at, :] += dot(ds, q_blk)
            dq_t = dq_t + dot(k_t[:, k_at], ds)
        dq_t = (dq_t * ATTN_SCALE).astype(jnp.bfloat16)
        dqs[at_q, :HEAD] = dq_t[:, :BLOCK].T
        dqs[at_q, HEAD:] = dq_t[:, BLOCK:].T
        return carry

    lax.fori_loop(0, qs.shape[0] // BLOCK, block, jnp.int32(0))

    for at in range(n_do):
        o_out[at][...] = os[piece_at(at // n_mp, at % n_mp), :]
    dq_same[...] = dqs[same, :]
    dq_oth[...] = dqs[oth, :]
    for out, at in ((dkv_same, same_kv), (dkv_oth, oth_kv), (dh_same, same), (dh_oth, oth)):
        out[:, :HEAD] = (dk[at, :] * ATTN_SCALE).astype(out.dtype)
        out[:, HEAD:] = dv[at, :].astype(out.dtype)


def attention(n_mp, rows, chunk, heads_core, heads_chunk, place, opened, lo, near, halo, grads):
    heads_mp = 2 * heads_core
    piece = rows // n_mp
    pair = GROUP * HEAD

    def at_head(g, sc, *unused):
        return (0, sc[0] * heads_core + chunk * heads_chunk + g)

    def at_grad(g, sc, *unused):
        return (0, sc[1] * heads_mp + sc[0] * heads_core + chunk * heads_chunk + g)

    def at_local(g, *unused):
        return (0, g)

    in_specs = [pl.BlockSpec((1, 2 * rows), lambda g, *unused: (0, 0))]
    in_specs += [pl.BlockSpec((rows, pair), at_head)] * 2
    in_specs += [pl.BlockSpec((rows, HEAD), at_head)] * 4
    in_specs += [pl.BlockSpec((rows, pair), at_local)] * 2
    in_specs += [pl.BlockSpec((piece, pair), at_grad)]
    in_specs += [pl.BlockSpec((piece, pair), at_local)] * (2 * n_mp - 1)
    out_specs = [pl.BlockSpec((piece, pair), at_local)] * (2 * n_mp)
    out_specs += [pl.BlockSpec((rows, pair), at_local)] * 6
    wide = heads_chunk * pair
    bf, f32 = jnp.bfloat16, jnp.float32
    out_shape = [jax.ShapeDtypeStruct((piece, wide), bf)] * (2 * n_mp)
    out_shape += [jax.ShapeDtypeStruct((rows, wide), t) for t in (bf, bf, f32, bf, bf, bf)]
    tokens, keys, slab = 2 * rows, WINDOW + 2 * rows, SPAN * BLOCK
    flops = heads_chunk * 6 * 2 * GROUP * tokens * slab * HEAD
    return pl.pallas_call(
        functools.partial(attention_kernel, n_mp, rows),
        grid_spec=pltpu.PrefetchScalarGridSpec(
            num_scalar_prefetch=2,
            grid=(heads_chunk,),
            in_specs=in_specs,
            out_specs=out_specs,
            scratch_shapes=[
                pltpu.VMEM((tokens, pair), bf),
                pltpu.VMEM((keys, HEAD), bf),
                pltpu.VMEM((keys, HEAD), bf),
                pltpu.VMEM((HEAD, keys), bf),
                pltpu.VMEM((HEAD, keys), bf),
                pltpu.VMEM((tokens, pair), bf),
                pltpu.VMEM((tokens, pair), bf),
                pltpu.VMEM((tokens, pair), bf),
                pltpu.VMEM((keys, HEAD), f32),
                pltpu.VMEM((keys, HEAD), f32),
                pltpu.VMEM((slab, GROUP * BLOCK), f32),
                pltpu.VMEM((slab, GROUP * BLOCK), bf),
            ],
        ),
        out_shape=out_shape,
        compiler_params=pltpu.CompilerParams(
            dimension_semantics=("arbitrary",), vmem_limit_bytes=48 * 1024 * 1024
        ),
        cost_estimate=pl.CostEstimate(
            flops=flops,
            bytes_accessed=heads_chunk * 12 * rows * pair * 2,
            transcendentals=heads_chunk * GROUP * tokens * slab,
        ),
        name="attention",
    )(place, opened, lo, *near, *halo, *grads)


def sum_kernel(heads, sc_ref, *refs):
    near, far, dk_out, dv_out = refs[0], refs[1], refs[2], refs[3]


def body(queries, keys, values, grad_out, band_mask, segment_ids):
    n_ctx, n_mp = lax.axis_size("ctx"), lax.axis_size("mp")
    rows = queries.shape[0]
    piece = rows // n_mp
    heads_mp = KV_HEADS // n_mp
    heads_core = heads_mp // 2
    heads_chunk = heads_core // CHUNKS
    pair = GROUP * HEAD
    wide = heads_chunk * pair
    bf = jnp.bfloat16
    ctx, mp = lax.axis_index("ctx"), lax.axis_index("mp")
    core, chip = lax.rem(ctx, 2), ctx // 2
    place = jnp.stack([core, mp]).astype(jnp.int32)

    def send(x, target):
        return lax.ppermute(x, AXES, routes(target, n_ctx, n_mp))

    def plan_halo(core, mp):
        jobs = []
        for i in range(CHUNKS):
            for side in range(2):
                half = core if side == 0 else 1 - core
                for g in range(heads_chunk):
                    at = pl.multiple_of((half * heads_core + i * heads_chunk + g) * HEAD, HEAD)
                    for which in range(2):
                        jobs.append(
                            (which, at, 2 * i + side, g * pair + which * HEAD, rows, HEAD)
                        )
        return jobs

    halos = run_copies(
        plan_halo,
        place,
        (keys, values),
        [jax.ShapeDtypeStruct((rows, wide), bf)] * (2 * CHUNKS),
        2 * CHUNKS * heads_chunk * 2,
    )
    partners = [(dk, dm) for dk in range(2) for dm in range(n_mp)]

    def plan_grad(core, mp):
        jobs = []
        for i in range(CHUNKS):
            for at, (dk, dm) in enumerate(partners[1:]):
                core_to = core if dk == 0 else 1 - core
                mp_to = lax.rem(mp + dm, n_mp)
                col = (mp_to * heads_mp + core_to * heads_core + i * heads_chunk) * pair
                jobs.append(
                    (0, pl.multiple_of(col, HEAD), i * (2 * n_mp - 1) + at, 0, piece, wide)
                )
        return jobs

    sent_grads = run_copies(
        plan_grad,
        place,
        (grad_out,),
        [jax.ShapeDtypeStruct((piece, wide), bf)] * (CHUNKS * (2 * n_mp - 1)),
        CHUNKS * (2 * n_mp - 1),
    )

    halo_in, grads_in = [], []
    for i in range(CHUNKS):
        halo_in.append(
            (
                send(halos[2 * i], lambda c, m: (c + 2, m)),
                send(halos[2 * i + 1], lambda c, m: ((c + 2) ^ 1, m)),
            )
        )
        grads_in.append(
            [
                send(sent_grads[i * (2 * n_mp - 1) + at], lambda c, m: (c ^ dk, (m + dm) % n_mp))
                for at, (dk, dm) in enumerate(partners[1:])
            ]
        )
    swap = lambda c, m: (c ^ 1, m)
    near = (
        queries,
        send(queries, swap),
        keys,
        send(keys, swap),
        values,
        send(values, swap),
    )

    tokens = 2 * rows
    padded = jnp.concatenate([jnp.full((WINDOW,), -1, jnp.int32), segment_ids])
    ids = lax.dynamic_slice_in_dim(padded, chip * tokens, WINDOW + tokens, 0)
    before = jnp.sum((ids[:, None] < ids[None, WINDOW:]).astype(jnp.int32), axis=0)
    lo = jnp.maximum(before, jnp.arange(1, tokens + 1, dtype=jnp.int32))[None, :]
    blocks = tokens // BLOCK
    opened = lax.dynamic_slice_in_dim(band_mask, chip * blocks, blocks, 0).reshape(-1)

    out_parts, dq_parts, near_parts, far_parts = [], [], [], []
    for i in range(CHUNKS):
        done = attention(
            n_mp,
            rows,
            i,
            heads_core,
            heads_chunk,
            place,
            opened,
            lo,
            near,
            halo_in[i],
            [grad_out] + grads_in[i],
        )
        o_pieces = done[: 2 * n_mp]
        dq_same, dq_oth, dkv_same, dkv_oth, dh_same, dh_oth = done[2 * n_mp :]
        back_same = send(dh_same, lambda c, m: (c - 2, m))
        back_oth = send(dh_oth, lambda c, m: ((c - 2) ^ 1 if c >= 2 else -1, m))
        out_parts.append(
            [o_pieces[0]]
            + [
                send(o_pieces[1 + at], lambda c, m: (c ^ dk, (m + dm) % n_mp))
                for at, (dk, dm) in enumerate(partners[1:])
            ]
        )
        dq_parts.append((dq_same, send(dq_oth, swap)))
        near_parts.append((dkv_same, send(dkv_oth, swap)))
        far_parts.append((back_same, back_oth))

    arrays = [x for part in out_parts for x in part] + [x for part in dq_parts for x in part]

    def plan_out(core, mp):
        jobs = []
        for i in range(CHUNKS):
            for at, (dk, dm) in enumerate(partners):
                core_from = core if dk == 0 else 1 - core
                mp_from = lax.rem(mp + n_mp - dm, n_mp)
                col = (mp_from * heads_mp + core_from * heads_core + i * heads_chunk) * pair
                jobs.append((i * 2 * n_mp + at, 0, 0, pl.multiple_of(col, HEAD), piece, wide))
        for i in range(CHUNKS):
            for side in range(2):
                half = core if side == 0 else 1 - core
                col = (half * heads_core + i * heads_chunk) * pair
                src = CHUNKS * 2 * n_mp + 2 * i + side
                jobs.append((src, 0, 1, pl.multiple_of(col, HEAD), rows, wide))
        return jobs

    attn_out, grad_queries = run_copies(
        plan_out,
        place,
        arrays,
        [
            jax.ShapeDtypeStruct((piece, n_mp * heads_mp * pair), bf),
            jax.ShapeDtypeStruct(queries.shape, bf),
        ],
        len(arrays),
    )

    def halves(pairs):
        same = jnp.concatenate([p[0].astype(jnp.float32) for p in pairs], axis=1)
        oth = jnp.concatenate([p[1].astype(jnp.float32) for p in pairs], axis=1)
        return same, oth

    near_same, near_oth = halves(near_parts)
    far_same, far_oth = halves(far_parts)
    same, oth = near_same + far_same, near_oth + far_oth
    low = jnp.where(core == 0, same, oth).astype(bf)
    high = jnp.where(core == 0, oth, same).astype(bf)
    both = jnp.concatenate([low, high], axis=1).reshape(rows, heads_mp, 2, HEAD)
    grad_keys = both[:, :, 0].reshape(rows, heads_mp * HEAD)
    grad_values = both[:, :, 1].reshape(rows, heads_mp * HEAD)
    return attn_out, grad_queries, grad_keys, grad_values


def solution(mesh):
    placed = (P("ctx", "mp"), P("ctx", "mp"), P("ctx", "mp"), P(("ctx", "mp"), None), P(), P())
    return jax.shard_map(
        body,
        mesh=mesh,
        in_specs=placed,
        out_specs=(P(("ctx", "mp"), None), P("ctx", "mp"), P("ctx", "mp"), P("ctx", "mp")),
        check_vma=False,
    )
```

```python
import functools
import math

import jax
import jax.numpy as jnp
from jax import lax
from jax.experimental import pallas as pl
from jax.experimental.pallas import tpu as pltpu
from jax.sharding import PartitionSpec as P

KV_HEADS = 16
GROUP = 2
HEAD = 128
WINDOW = 1024
BLOCK = 128
SPAN = WINDOW // BLOCK + 1
CHUNKS = 2
ATTN_SCALE = 168.0 ** (-0.5)
EXP2_SCALE = ATTN_SCALE * math.log2(math.e)
MASKED = -1e30
FAR = 1 << 20
AXES = ("ctx", "mp")
NT = (((1,), (1,)), ((), ()))
NN = (((1,), (0,)), ((), ()))


def dot(a, b, dims=NN):
    return lax.dot_general(a, b, dims, preferred_element_type=jnp.float32)


def routes(target, n_ctx, n_mp):
    out = []
    for c in range(n_ctx):
        for m in range(n_mp):
            d = target(c, m)
            if 0 <= d[0] < n_ctx:
                out.append((c * n_mp + m, d[0] * n_mp + d[1]))
    return out


def pack_halo_kernel(sc_ref, k_same, v_same, k_oth, v_oth, same, oth):
    same[:, :HEAD] = k_same[...]
    same[:, HEAD:] = v_same[...]
    oth[:, :HEAD] = k_oth[...]
    oth[:, HEAD:] = v_oth[...]


def pack_halo(place, keys, values, chunk, heads_core, heads_chunk):
    rows, pair = keys.shape[0], 2 * HEAD

    def at_half(side):
        def index(g, sc):
            half = sc[0] if side == 0 else 1 - sc[0]
            return (0, half * heads_core + chunk * heads_chunk + g)

        return index

    return pl.pallas_call(
        pack_halo_kernel,
        grid_spec=pltpu.PrefetchScalarGridSpec(
            num_scalar_prefetch=1,
            grid=(heads_chunk,),
            in_specs=[pl.BlockSpec((rows, HEAD), at_half(n // 2)) for n in range(4)],
            out_specs=[pl.BlockSpec((rows, pair), lambda g, sc: (0, g))] * 2,
        ),
        out_shape=[jax.ShapeDtypeStruct((rows, heads_chunk * pair), keys.dtype)] * 2,
        cost_estimate=pl.CostEstimate(
            flops=0, bytes_accessed=8 * rows * heads_chunk * pair, transcendentals=0
        ),
        name="pack_halo",
    )(place, keys, values, keys, values)


def pack_grad_kernel(n, sc_ref, *refs):
    for at in range(n):
        refs[n + at][...] = refs[at][...]


def pack_grad(place, grad_out, chunk, heads_core, heads_chunk, n_mp, partners):
    piece, pair = grad_out.shape[0], GROUP * HEAD

    def at_partner(dk, dm):
        def index(g, sc):
            core = sc[0] if dk == 0 else 1 - sc[0]
            mp = lax.rem(sc[1] + dm, n_mp)
            return (0, (mp * 2 + core) * heads_core + chunk * heads_chunk + g)

        return index

    n = len(partners)
    return pl.pallas_call(
        functools.partial(pack_grad_kernel, n),
        grid_spec=pltpu.PrefetchScalarGridSpec(
            num_scalar_prefetch=1,
            grid=(heads_chunk,),
            in_specs=[pl.BlockSpec((piece, pair), at_partner(*p)) for p in partners],
            out_specs=[pl.BlockSpec((piece, pair), lambda g, sc: (0, g))] * n,
        ),
        out_shape=[jax.ShapeDtypeStruct((piece, heads_chunk * pair), grad_out.dtype)] * n,
        cost_estimate=pl.CostEstimate(
            flops=0, bytes_accessed=4 * n * piece * heads_chunk * pair, transcendentals=0
        ),
        name="pack_grad",
    )(place, *[grad_out] * n)


def place_kernel(jobs, n_in, sc_ref, *refs):
    for src, dst, width, column in jobs:
        col = pl.multiple_of(column(sc_ref[0], sc_ref[1]), HEAD)
        refs[n_in + dst][:, pl.ds(col, width)] = refs[src][...]


def place_columns(place, arrays, outs, jobs):
    vmem = pl.BlockSpec(memory_space=pltpu.VMEM)
    moved = sum(math.prod(o.shape) * o.dtype.itemsize for o in outs)
    return pl.pallas_call(
        functools.partial(place_kernel, jobs, len(arrays)),
        in_specs=[pl.BlockSpec(memory_space=pltpu.SMEM)] + [vmem] * len(arrays),
        out_specs=[vmem] * len(outs),
        out_shape=outs,
        compiler_params=pltpu.CompilerParams(vmem_limit_bytes=32 * 1024 * 1024),
        cost_estimate=pl.CostEstimate(flops=0, bytes_accessed=2 * moved, transcendentals=0),
        name="place_columns",
    )(place, *arrays)


def sum_kernel(sc_ref, near_same, far_same, near_oth, far_oth, *refs):
    dk, dv = refs[-2:]

    @pl.when(pl.program_id(0) == 0)
    def _():
        total = near_same[...] + far_same[...].astype(jnp.float32)
        dk[...] = total[:, :HEAD].astype(dk.dtype)
        dv[...] = total[:, HEAD:].astype(dv.dtype)

    @pl.when(pl.program_id(0) == 1)
    def _():
        total = near_oth[...].astype(jnp.float32) + far_oth[...].astype(jnp.float32)
        dk[...] = total[:, :HEAD].astype(dk.dtype)
        dv[...] = total[:, HEAD:].astype(dv.dtype)


def sum_terms(place, chunk, heads_core, heads_chunk, terms, before):
    rows, pair = terms[0].shape[0], 2 * HEAD
    last = heads_chunk - 1

    def at_same(side, g, sc):
        return (0, jnp.where(side == 0, g, last))

    def at_oth(side, g, sc):
        return (0, jnp.where(side == 1, g, 0))

    def at_out(side, g, sc):
        half = jnp.where(side == 0, sc[0], 1 - sc[0])
        return (0, half * heads_core + chunk * heads_chunk + g)

    shape = jax.ShapeDtypeStruct((rows, 2 * heads_core * HEAD), jnp.bfloat16)
    in_specs = [pl.BlockSpec((rows, pair), at) for at in (at_same, at_same, at_oth, at_oth)]
    return pl.pallas_call(
        sum_kernel,
        grid_spec=pltpu.PrefetchScalarGridSpec(
            num_scalar_prefetch=1,
            grid=(2, heads_chunk),
            in_specs=in_specs + [pl.BlockSpec(memory_space=pl.ANY)] * len(before),
            out_specs=[pl.BlockSpec((rows, HEAD), at_out)] * 2,
        ),
        out_shape=[shape, shape],
        input_output_aliases={5: 0, 6: 1} if before else {},
        cost_estimate=pl.CostEstimate(
            flops=0, bytes_accessed=14 * rows * heads_chunk * pair, transcendentals=0
        ),
        name="sum_terms",
    )(place, *terms, *before)


def attention_kernel(n_mp, rows, sc_ref, open_ref, lo_ref, *refs):
    n_do = 2 * n_mp
    q_own, q_oth, k_own, k_oth, v_own, v_oth, h_same, h_oth = refs[:8]
    do_in = refs[8 : 8 + n_do]
    outs = refs[8 + n_do : 8 + 2 * n_do + 6]
    o_out = outs[:n_do]
    dq_same, dq_oth, dkv_same, dkv_oth, dh_same, dh_oth = outs[n_do:]
    qs, ks, vs, k_t, v_t, dos, os, dqs, dk, dv, s_ref, e_ref = refs[8 + 2 * n_do + 6 :]
    core, mp = sc_ref[0], sc_ref[1]
    piece = rows // n_mp
    same = pl.ds(pl.multiple_of(core * rows, rows), rows)
    oth = pl.ds(pl.multiple_of((1 - core) * rows, rows), rows)
    same_kv = pl.ds(pl.multiple_of(WINDOW + core * rows, rows), rows)
    oth_kv = pl.ds(pl.multiple_of(WINDOW + (1 - core) * rows, rows), rows)

    def piece_at(dk_, dm):
        k_at = core if dk_ == 0 else 1 - core
        return pl.ds(pl.multiple_of(k_at * rows + lax.rem(mp + dm, n_mp) * piece, piece), piece)

    qs[same, :] = q_own[...]
    qs[oth, :] = q_oth[...]
    ks[same, :] = h_same[:, :HEAD]
    ks[oth, :] = h_oth[:, :HEAD]
    ks[same_kv, :] = k_own[...]
    ks[oth_kv, :] = k_oth[...]
    vs[same, :] = h_same[:, HEAD:]
    vs[oth, :] = h_oth[:, HEAD:]
    vs[same_kv, :] = v_own[...]
    vs[oth_kv, :] = v_oth[...]
    for at in range(n_do):
        dos[piece_at(at // n_mp, n_mp - at % n_mp), :] = do_in[at][...]
    dk[...] = jnp.zeros_like(dk)
    dv[...] = jnp.zeros_like(dv)
    for t in range(ks.shape[0] // 256):
        at = slice(t * 256, t * 256 + 256)
        k_t[:, at] = ks[at, :].T
        v_t[:, at] = vs[at, :].T

    row = lax.broadcasted_iota(jnp.int32, (BLOCK, GROUP * BLOCK), 0)
    lane = lax.broadcasted_iota(jnp.int32, (BLOCK, GROUP * BLOCK), 1)
    causal = row <= lax.rem(lane, BLOCK)

    def block(b, carry):
        at_q = pl.ds(pl.multiple_of(b * BLOCK, BLOCK), BLOCK)
        q_blk = jnp.concatenate([qs[at_q, :HEAD], qs[at_q, HEAD:]], axis=0)
        lo = lo_ref[:, at_q]
        lo = jnp.concatenate([lo, lo], axis=1)
        top = jnp.full((8, GROUP * BLOCK), MASKED, jnp.float32)
        for j in range(SPAN):
            k_at = pl.ds(pl.multiple_of((b + j) * BLOCK, BLOCK), BLOCK)
            part = slice(j * BLOCK, j * BLOCK + BLOCK)
            s = dot(ks[k_at, :], q_blk, NT)
            closed = jnp.where(open_ref[b * SPAN + SPAN - 1 - j] == 1, 0, FAR)
            valid = row >= jnp.maximum(lo - (b + j) * BLOCK, closed)
            if j == SPAN - 1:
                valid = valid & causal
            s = jnp.where(valid, s, MASKED)
            s_ref[part, :] = s
            top = jnp.maximum(top, jnp.max(s.reshape(BLOCK // 8, 8, GROUP * BLOCK), axis=0))
        top = jnp.max(top, axis=0, keepdims=True)
        total = jnp.zeros((8, GROUP * BLOCK), jnp.float32)
        for j in range(SPAN):
            part = slice(j * BLOCK, j * BLOCK + BLOCK)
            e = jnp.exp2((s_ref[part, :] - top) * EXP2_SCALE)
            total = total + jnp.sum(e.reshape(BLOCK // 8, 8, GROUP * BLOCK), axis=0)
            e_ref[part, :] = e.astype(jnp.bfloat16)
        inverse = 1.0 / jnp.sum(total, axis=0, keepdims=True)
        at_keys = pl.ds(pl.multiple_of(b * BLOCK, BLOCK), SPAN * BLOCK)
        o_t = (dot(v_t[:, at_keys], e_ref[...]) * inverse).astype(jnp.bfloat16)
        os[at_q, :HEAD] = o_t[:, :BLOCK].T
        os[at_q, HEAD:] = o_t[:, BLOCK:].T
        do_t = jnp.concatenate([dos[at_q, :HEAD].T, dos[at_q, HEAD:].T], axis=1)
        do_t = (do_t.astype(jnp.float32) * inverse).astype(jnp.bfloat16)
        delta = jnp.sum(
            do_t.astype(jnp.float32) * o_t.astype(jnp.float32), axis=0, keepdims=True
        )
        dq_t = jnp.zeros((HEAD, GROUP * BLOCK), jnp.float32)
        for j in range(SPAN):
            k_at = pl.ds(pl.multiple_of((b + j) * BLOCK, BLOCK), BLOCK)
            part = slice(j * BLOCK, j * BLOCK + BLOCK)
            dp = dot(vs[k_at, :], do_t)
            e = e_ref[part, :]
            ds = (e.astype(jnp.float32) * (dp - delta)).astype(jnp.bfloat16)
            dv[k_at, :] += dot(e, do_t, NT)
            dk[k_at, :] += dot(ds, q_blk)
            dq_t = dq_t + dot(k_t[:, k_at], ds)
        dq_t = (dq_t * ATTN_SCALE).astype(jnp.bfloat16)
        dqs[at_q, :HEAD] = dq_t[:, :BLOCK].T
        dqs[at_q, HEAD:] = dq_t[:, BLOCK:].T
        return carry

    lax.fori_loop(0, qs.shape[0] // BLOCK, block, jnp.int32(0))

    for at in range(n_do):
        o_out[at][...] = os[piece_at(at // n_mp, at % n_mp), :]
    dq_same[...] = dqs[same, :]
    dq_oth[...] = dqs[oth, :]
    for out, at in ((dkv_same, same_kv), (dkv_oth, oth_kv), (dh_same, same), (dh_oth, oth)):
        out[:, :HEAD] = (dk[at, :] * ATTN_SCALE).astype(out.dtype)
        out[:, HEAD:] = dv[at, :].astype(out.dtype)


def attention(n_mp, rows, chunk, heads_core, heads_chunk, place, opened, lo, near, halo, grads):
    heads_mp = 2 * heads_core
    piece = rows // n_mp
    pair = GROUP * HEAD

    def at_head(g, sc, *unused):
        return (0, sc[0] * heads_core + chunk * heads_chunk + g)

    def at_grad(g, sc, *unused):
        return (0, sc[1] * heads_mp + sc[0] * heads_core + chunk * heads_chunk + g)

    def at_local(g, *unused):
        return (0, g)

    in_specs = [pl.BlockSpec((1, 2 * rows), lambda g, *unused: (0, 0))]
    in_specs += [pl.BlockSpec((rows, pair), at_head)] * 2
    in_specs += [pl.BlockSpec((rows, HEAD), at_head)] * 4
    in_specs += [pl.BlockSpec((rows, pair), at_local)] * 2
    in_specs += [pl.BlockSpec((piece, pair), at_grad)]
    in_specs += [pl.BlockSpec((piece, pair), at_local)] * (2 * n_mp - 1)
    out_specs = [pl.BlockSpec((piece, pair), at_local)] * (2 * n_mp)
    out_specs += [pl.BlockSpec((rows, pair), at_local)] * 6
    wide = heads_chunk * pair
    bf, f32 = jnp.bfloat16, jnp.float32
    out_shape = [jax.ShapeDtypeStruct((piece, wide), bf)] * (2 * n_mp)
    out_shape += [jax.ShapeDtypeStruct((rows, wide), t) for t in (bf, bf, f32, bf, bf, bf)]
    tokens, keys, slab = 2 * rows, WINDOW + 2 * rows, SPAN * BLOCK
    flops = heads_chunk * 6 * 2 * GROUP * tokens * slab * HEAD
    return pl.pallas_call(
        functools.partial(attention_kernel, n_mp, rows),
        grid_spec=pltpu.PrefetchScalarGridSpec(
            num_scalar_prefetch=2,
            grid=(heads_chunk,),
            in_specs=in_specs,
            out_specs=out_specs,
            scratch_shapes=[
                pltpu.VMEM((tokens, pair), bf),
                pltpu.VMEM((keys, HEAD), bf),
                pltpu.VMEM((keys, HEAD), bf),
                pltpu.VMEM((HEAD, keys), bf),
                pltpu.VMEM((HEAD, keys), bf),
                pltpu.VMEM((tokens, pair), bf),
                pltpu.VMEM((tokens, pair), bf),
                pltpu.VMEM((tokens, pair), bf),
                pltpu.VMEM((keys, HEAD), f32),
                pltpu.VMEM((keys, HEAD), f32),
                pltpu.VMEM((slab, GROUP * BLOCK), f32),
                pltpu.VMEM((slab, GROUP * BLOCK), bf),
            ],
        ),
        out_shape=out_shape,
        compiler_params=pltpu.CompilerParams(
            dimension_semantics=("arbitrary",), vmem_limit_bytes=48 * 1024 * 1024
        ),
        cost_estimate=pl.CostEstimate(
            flops=flops,
            bytes_accessed=heads_chunk * 12 * rows * pair * 2,
            transcendentals=heads_chunk * GROUP * tokens * slab,
        ),
        name="attention",
    )(place, opened, lo, *near, *halo, *grads)


def body(queries, keys, values, grad_out, band_mask, segment_ids):
    n_ctx, n_mp = lax.axis_size("ctx"), lax.axis_size("mp")
    rows = queries.shape[0]
    piece = rows // n_mp
    heads_mp = KV_HEADS // n_mp
    heads_core = heads_mp // 2
    heads_chunk = heads_core // CHUNKS
    pair = GROUP * HEAD
    wide = heads_chunk * pair
    bf = jnp.bfloat16
    ctx, mp = lax.axis_index("ctx"), lax.axis_index("mp")
    core, chip = lax.rem(ctx, 2), ctx // 2
    place = jnp.stack([core, mp]).astype(jnp.int32)

    def send(x, target):
        return lax.ppermute(x, AXES, routes(target, n_ctx, n_mp))

    partners = [(dk, dm) for dk in range(2) for dm in range(n_mp)]
    halo_in, grads_in = [], []
    for i in range(CHUNKS):
        halo_same, halo_oth = pack_halo(place, keys, values, i, heads_core, heads_chunk)
        halo_in.append(
            (
                send(halo_same, lambda c, m: (c + 2, m)),
                send(halo_oth, lambda c, m: ((c + 2) ^ 1, m)),
            )
        )
        sent = pack_grad(place, grad_out, i, heads_core, heads_chunk, n_mp, partners[1:])
        grads_in.append(
            [
                send(sent[at], lambda c, m: (c ^ dk, (m + dm) % n_mp))
                for at, (dk, dm) in enumerate(partners[1:])
            ]
        )
    swap = lambda c, m: (c ^ 1, m)
    near = (
        queries,
        send(queries, swap),
        keys,
        send(keys, swap),
        values,
        send(values, swap),
    )

    tokens = 2 * rows
    padded = jnp.concatenate([jnp.full((WINDOW,), -1, jnp.int32), segment_ids])
    ids = lax.dynamic_slice_in_dim(padded, chip * tokens, WINDOW + tokens, 0)
    before = jnp.sum((ids[:, None] < ids[None, WINDOW:]).astype(jnp.int32), axis=0)
    lo = jnp.maximum(before, jnp.arange(1, tokens + 1, dtype=jnp.int32))[None, :]
    blocks = tokens // BLOCK
    opened = lax.dynamic_slice_in_dim(band_mask, chip * blocks, blocks, 0).reshape(-1)

    out_parts, dq_parts, near_parts, far_parts = [], [], [], []
    for i in range(CHUNKS):
        done = attention(
            n_mp,
            rows,
            i,
            heads_core,
            heads_chunk,
            place,
            opened,
            lo,
            near,
            halo_in[i],
            [grad_out] + grads_in[i],
        )
        o_pieces = done[: 2 * n_mp]
        dq_same, dq_oth, dkv_same, dkv_oth, dh_same, dh_oth = done[2 * n_mp :]
        back_same = send(dh_same, lambda c, m: (c - 2, m))
        back_oth = send(dh_oth, lambda c, m: ((c - 2) ^ 1 if c >= 2 else -1, m))
        out_parts.append(
            [o_pieces[0]]
            + [
                send(o_pieces[1 + at], lambda c, m: (c ^ dk, (m + dm) % n_mp))
                for at, (dk, dm) in enumerate(partners[1:])
            ]
        )
        dq_parts.append((dq_same, send(dq_oth, swap)))
        near_parts.append((dkv_same, send(dkv_oth, swap)))
        far_parts.append((back_same, back_oth))

    def out_column(chunk, dk, dm):
        def column(core, mp):
            core_from = core if dk == 0 else 1 - core
            mp_from = lax.rem(mp + n_mp - dm, n_mp)
            return ((mp_from * 2 + core_from) * heads_core + chunk * heads_chunk) * pair

        return column

    def query_column(chunk, side):
        def column(core, mp):
            half = core if side == 0 else 1 - core
            return (half * heads_core + chunk * heads_chunk) * pair

        return column

    arrays, jobs = [], []
    for i in range(CHUNKS):
        for at, (dk, dm) in enumerate(partners):
            jobs.append((len(arrays), 0, wide, out_column(i, dk, dm)))
            arrays.append(out_parts[i][at])
        for side in range(2):
            jobs.append((len(arrays), 1, wide, query_column(i, side)))
            arrays.append(dq_parts[i][side])
    attn_out, grad_queries = place_columns(
        place,
        arrays,
        [
            jax.ShapeDtypeStruct((piece, n_mp * heads_mp * pair), bf),
            jax.ShapeDtypeStruct(queries.shape, bf),
        ],
        jobs,
    )

    grads_kv = ()
    for i in range(CHUNKS):
        terms = (near_parts[i][0], far_parts[i][0], near_parts[i][1], far_parts[i][1])
        grads_kv = sum_terms(place, i, heads_core, heads_chunk, terms, grads_kv)
    return attn_out, grad_queries, grads_kv[0], grads_kv[1]


def solution(mesh):
    placed = (P("ctx", "mp"), P("ctx", "mp"), P("ctx", "mp"), P(("ctx", "mp"), None), P(), P())
    return jax.shard_map(
        body,
        mesh=mesh,
        in_specs=placed,
        out_specs=(P(("ctx", "mp"), None), P("ctx", "mp"), P("ctx", "mp"), P("ctx", "mp")),
        check_vma=False,
    )
```

```python
import functools
import math

import jax
import jax.numpy as jnp
from jax import lax
from jax.experimental import pallas as pl
from jax.experimental.pallas import tpu as pltpu
from jax.sharding import PartitionSpec as P

KV_HEADS = 16
GROUP = 2
HEAD = 128
WINDOW = 1024
BLOCK = 128
SPAN = WINDOW // BLOCK + 1
CHUNKS = 2
ATTN_SCALE = 168.0 ** (-0.5)
EXP2_SCALE = ATTN_SCALE * math.log2(math.e)
MASKED = -1e30
FAR = 1 << 20
AXES = ("ctx", "mp")
NT = (((1,), (1,)), ((), ()))
NN = (((1,), (0,)), ((), ()))
LIGHT = pl.CostEstimate(flops=0, bytes_accessed=1024, transcendentals=0)
HEAVY = pl.CostEstimate(flops=25_000_000_000, bytes_accessed=1024, transcendentals=0)


def dot(a, b, dims=NN):
    return lax.dot_general(a, b, dims, preferred_element_type=jnp.float32)


def routes(target, n_ctx, n_mp):
    out = []
    for c in range(n_ctx):
        for m in range(n_mp):
            d = target(c, m)
            if 0 <= d[0] < n_ctx:
                out.append((c * n_mp + m, d[0] * n_mp + d[1]))
    return out


def pack_kernel(joins, n_after, sc_ref, *refs):
    outs = refs[sum(n for n, _ in joins) + n_after :]
    at = 0
    for out, (n, axis) in zip(outs, joins):
        out[...] = jnp.concatenate([ref[...] for ref in refs[at : at + n]], axis=axis)
        at += n


def pack(place, steps, inputs, outputs, after=(), name="pack"):
    flat = [i for group in inputs for i in group]
    joins = [(len(group), out[3]) for group, out in zip(inputs, outputs)]
    hbm = pl.BlockSpec(memory_space=pl.ANY)
    return pl.pallas_call(
        functools.partial(pack_kernel, joins, len(after)),
        grid_spec=pltpu.PrefetchScalarGridSpec(
            num_scalar_prefetch=1,
            grid=(steps,),
            in_specs=[pl.BlockSpec(i[1], i[2]) for i in flat] + [hbm] * len(after),
            out_specs=[pl.BlockSpec(o[1], o[2]) for o in outputs],
        ),
        out_shape=[jax.ShapeDtypeStruct(o[0], jnp.bfloat16) for o in outputs],
        cost_estimate=LIGHT,
        name=name,
    )(place, *[i[0] for i in flat], *after)


def place_kernel(jobs, n_in, sc_ref, *refs):
    for src, rows, src_col, dst, width, column in jobs:
        col = pl.multiple_of(column(sc_ref[0], sc_ref[1]), HEAD)
        at = pl.ds(pl.multiple_of(sc_ref[1] * rows, rows), rows) if rows else slice(None)
        refs[n_in + dst][:, pl.ds(col, width)] = refs[src][at, src_col : src_col + width]


def place_columns(place, arrays, outs, jobs):
    vmem = pl.BlockSpec(memory_space=pltpu.VMEM)
    moved = sum(math.prod(o.shape) * o.dtype.itemsize for o in outs)
    return pl.pallas_call(
        functools.partial(place_kernel, jobs, len(arrays)),
        in_specs=[pl.BlockSpec(memory_space=pltpu.SMEM)] + [vmem] * len(arrays),
        out_specs=[vmem] * len(outs),
        out_shape=outs,
        compiler_params=pltpu.CompilerParams(vmem_limit_bytes=32 * 1024 * 1024),
        cost_estimate=LIGHT,
        name="place_columns",
    )(place, *arrays)


def sum_kernel(sc_ref, near_same, far_same, near_oth, far_oth, *refs):
    dk, dv = refs[-2:]

    @pl.when(pl.program_id(0) == 0)
    def _():
        total = near_same[...] + far_same[...].astype(jnp.float32)
        dk[...] = total[:, :HEAD].astype(dk.dtype)
        dv[...] = total[:, HEAD:].astype(dv.dtype)

    @pl.when(pl.program_id(0) == 1)
    def _():
        total = near_oth[...].astype(jnp.float32) + far_oth[...].astype(jnp.float32)
        dk[...] = total[:, :HEAD].astype(dk.dtype)
        dv[...] = total[:, HEAD:].astype(dv.dtype)


def sum_terms(place, chunk, heads_core, heads_chunk, terms, before, after=()):
    rows, pair = terms[0].shape[0], 2 * HEAD
    last = heads_chunk - 1

    def at_same(side, g, sc):
        return (0, jnp.where(side == 0, g, last))

    def at_oth(side, g, sc):
        return (0, jnp.where(side == 1, g, 0))

    def at_across(side, g, sc):
        return (0, 3 * jnp.where(side == 1, g, 0) + 1)

    def at_out(side, g, sc):
        half = jnp.where(side == 0, sc[0], 1 - sc[0])
        return (0, half * heads_core + chunk * heads_chunk + g)

    shape = jax.ShapeDtypeStruct((rows, 2 * heads_core * HEAD), jnp.bfloat16)
    in_specs = [pl.BlockSpec((rows, pair), at) for at in (at_same, at_same, at_across, at_oth)]
    return pl.pallas_call(
        sum_kernel,
        grid_spec=pltpu.PrefetchScalarGridSpec(
            num_scalar_prefetch=1,
            grid=(2, heads_chunk),
            in_specs=in_specs + [pl.BlockSpec(memory_space=pl.ANY)] * len((*before, *after)),
            out_specs=[pl.BlockSpec((rows, HEAD), at_out)] * 2,
        ),
        out_shape=[shape, shape],
        input_output_aliases={5: 0, 6: 1} if before else {},
        cost_estimate=LIGHT,
        name="sum_terms",
    )(place, *terms, *before, *after)


def attention_kernel(n_mp, rows, sc_ref, open_ref, lo_ref, *refs):
    q_own, k_own, v_own, near, h_same, h_oth, do_own, do_oth = refs[:8]
    do_far = refs[8 : 7 + n_mp]
    refs = refs[7 + n_mp :]
    dq_same, dkv_same, dh_same, dh_oth, across, o_own = refs[:6]
    o_far = refs[6 : 4 + 2 * n_mp]
    qs, ks, vs, k_t, v_t, dos, os, dqs, dk, dv, s_ref, e_ref = refs[4 + 2 * n_mp :]
    core, mp = sc_ref[0], sc_ref[1]
    piece, pair = rows // n_mp, GROUP * HEAD
    same = pl.ds(pl.multiple_of(core * rows, rows), rows)
    oth = pl.ds(pl.multiple_of((1 - core) * rows, rows), rows)
    same_kv = pl.ds(pl.multiple_of(WINDOW + core * rows, rows), rows)
    oth_kv = pl.ds(pl.multiple_of(WINDOW + (1 - core) * rows, rows), rows)

    def piece_at(dk_, dm):
        k_at = core if dk_ == 0 else 1 - core
        return pl.ds(pl.multiple_of(k_at * rows + lax.rem(mp + dm, n_mp) * piece, piece), piece)

    qs[same, :] = q_own[...]
    qs[oth, :] = near[:, :pair]
    ks[same, :] = h_same[:, :HEAD]
    ks[oth, :] = h_oth[:, :HEAD]
    ks[same_kv, :] = k_own[...]
    ks[oth_kv, :] = near[:, pair : pair + HEAD]
    vs[same, :] = h_same[:, HEAD:]
    vs[oth, :] = h_oth[:, HEAD:]
    vs[same_kv, :] = v_own[...]
    vs[oth_kv, :] = near[:, pair + HEAD :]
    dos[piece_at(0, 0), :] = do_own[...]
    dos[piece_at(1, 0), :] = do_oth[...]
    for at in range(n_mp - 1):
        dos[piece_at(0, n_mp - 1 - at), :] = do_far[at][:piece, :]
        dos[piece_at(1, n_mp - 1 - at), :] = do_far[at][piece:, :]
    dk[...] = jnp.zeros_like(dk)
    dv[...] = jnp.zeros_like(dv)
    for t in range(ks.shape[0] // 256):
        at = slice(t * 256, t * 256 + 256)
        k_t[:, at] = ks[at, :].T
        v_t[:, at] = vs[at, :].T

    row = lax.broadcasted_iota(jnp.int32, (BLOCK, GROUP * BLOCK), 0)
    lane = lax.broadcasted_iota(jnp.int32, (BLOCK, GROUP * BLOCK), 1)
    causal = row <= lax.rem(lane, BLOCK)

    def block(b, carry):
        at_q = pl.ds(pl.multiple_of(b * BLOCK, BLOCK), BLOCK)
        q_blk = jnp.concatenate([qs[at_q, :HEAD], qs[at_q, HEAD:]], axis=0)
        lo = lo_ref[:, at_q]
        lo = jnp.concatenate([lo, lo], axis=1)
        top = jnp.full((8, GROUP * BLOCK), MASKED, jnp.float32)
        for j in range(SPAN):
            k_at = pl.ds(pl.multiple_of((b + j) * BLOCK, BLOCK), BLOCK)
            part = slice(j * BLOCK, j * BLOCK + BLOCK)
            s = dot(ks[k_at, :], q_blk, NT)
            closed = jnp.where(open_ref[b * SPAN + SPAN - 1 - j] == 1, 0, FAR)
            valid = row >= jnp.maximum(lo - (b + j) * BLOCK, closed)
            if j == SPAN - 1:
                valid = valid & causal
            s = jnp.where(valid, s, MASKED)
            s_ref[part, :] = s
            top = jnp.maximum(top, jnp.max(s.reshape(BLOCK // 8, 8, GROUP * BLOCK), axis=0))
        top = jnp.max(top, axis=0, keepdims=True)
        total = jnp.zeros((8, GROUP * BLOCK), jnp.float32)
        for j in range(SPAN):
            part = slice(j * BLOCK, j * BLOCK + BLOCK)
            e = jnp.exp2((s_ref[part, :] - top) * EXP2_SCALE)
            total = total + jnp.sum(e.reshape(BLOCK // 8, 8, GROUP * BLOCK), axis=0)
            e_ref[part, :] = e.astype(jnp.bfloat16)
        inverse = 1.0 / jnp.sum(total, axis=0, keepdims=True)
        at_keys = pl.ds(pl.multiple_of(b * BLOCK, BLOCK), SPAN * BLOCK)
        o_t = (dot(v_t[:, at_keys], e_ref[...]) * inverse).astype(jnp.bfloat16)
        os[at_q, :HEAD] = o_t[:, :BLOCK].T
        os[at_q, HEAD:] = o_t[:, BLOCK:].T
        do_t = jnp.concatenate([dos[at_q, :HEAD].T, dos[at_q, HEAD:].T], axis=1)
        do_t = (do_t.astype(jnp.float32) * inverse).astype(jnp.bfloat16)
        delta = jnp.sum(
            do_t.astype(jnp.float32) * o_t.astype(jnp.float32), axis=0, keepdims=True
        )
        dq_t = jnp.zeros((HEAD, GROUP * BLOCK), jnp.float32)
        for j in range(SPAN):
            k_at = pl.ds(pl.multiple_of((b + j) * BLOCK, BLOCK), BLOCK)
            part = slice(j * BLOCK, j * BLOCK + BLOCK)
            dp = dot(vs[k_at, :], do_t)
            e = e_ref[part, :]
            ds = (e.astype(jnp.float32) * (dp - delta)).astype(jnp.bfloat16)
            dv[k_at, :] += dot(e, do_t, NT)
            dk[k_at, :] += dot(ds, q_blk)
            dq_t = dq_t + dot(k_t[:, k_at], ds)
        dq_t = (dq_t * ATTN_SCALE).astype(jnp.bfloat16)
        dqs[at_q, :HEAD] = dq_t[:, :BLOCK].T
        dqs[at_q, HEAD:] = dq_t[:, BLOCK:].T
        return carry

    lax.fori_loop(0, qs.shape[0] // BLOCK, block, jnp.int32(0))

    dq_same[...] = dqs[same, :]
    across[:, :pair] = dqs[oth, :]
    across[:, 2 * pair :] = os[oth, :]
    o_own[...] = os[piece_at(0, 0), :]
    for at in range(n_mp - 1):
        o_far[2 * at][...] = os[piece_at(0, at + 1), :]
        o_far[2 * at + 1][...] = os[piece_at(1, at + 1), :]
    for out, at in ((dkv_same, same_kv), (dh_same, same), (dh_oth, oth)):
        out[:, :HEAD] = (dk[at, :] * ATTN_SCALE).astype(out.dtype)
        out[:, HEAD:] = dv[at, :].astype(out.dtype)
    across[:, pair : pair + HEAD] = (dk[oth_kv, :] * ATTN_SCALE).astype(across.dtype)
    across[:, pair + HEAD : 2 * pair] = dv[oth_kv, :].astype(across.dtype)


def attention(n_mp, rows, chunk, heads_core, heads_chunk, place, opened, lo, own, near, halo, near_do, far_do):
    heads_mp = 2 * heads_core
    piece, pair = rows // n_mp, GROUP * HEAD
    first = chunk * heads_chunk

    def at_head(g, sc, *unused):
        return (0, sc[0] * heads_core + first + g)

    def at_grad(g, sc, *unused):
        return (0, sc[1] * heads_mp + sc[0] * heads_core + first + g)

    def at_near(g, *unused):
        return (0, first + g)

    def at_near_do(g, sc, *unused):
        return (sc[1], first + g)

    def at_local(g, *unused):
        return (0, g)

    in_specs = [pl.BlockSpec((1, 2 * rows), lambda g, *unused: (0, 0))]
    in_specs += [pl.BlockSpec((rows, pair), at_head)]
    in_specs += [pl.BlockSpec((rows, HEAD), at_head)] * 2
    in_specs += [pl.BlockSpec((rows, 2 * pair), at_near)]
    in_specs += [pl.BlockSpec((rows, pair), at_local)] * 2
    in_specs += [pl.BlockSpec((piece, pair), at_grad), pl.BlockSpec((piece, pair), at_near_do)]
    in_specs += [pl.BlockSpec((2 * piece, pair), at_local)] * (n_mp - 1)
    wide = heads_chunk * pair
    bf, f32 = jnp.bfloat16, jnp.float32
    out_specs = [pl.BlockSpec((rows, pair), at_local)] * 4
    out_specs += [pl.BlockSpec((rows, 3 * pair), at_local)]
    out_specs += [pl.BlockSpec((piece, pair), at_local)] * (2 * n_mp - 1)
    out_shape = [jax.ShapeDtypeStruct((rows, wide), t) for t in (bf, f32, bf, bf)]
    out_shape += [jax.ShapeDtypeStruct((rows, 3 * wide), bf)]
    out_shape += [jax.ShapeDtypeStruct((piece, wide), bf)] * (2 * n_mp - 1)
    tokens, keys, slab = 2 * rows, WINDOW + 2 * rows, SPAN * BLOCK
    return pl.pallas_call(
        functools.partial(attention_kernel, n_mp, rows),
        grid_spec=pltpu.PrefetchScalarGridSpec(
            num_scalar_prefetch=2,
            grid=(heads_chunk,),
            in_specs=in_specs,
            out_specs=out_specs,
            scratch_shapes=[
                pltpu.VMEM((tokens, pair), bf),
                pltpu.VMEM((keys, HEAD), bf),
                pltpu.VMEM((keys, HEAD), bf),
                pltpu.VMEM((HEAD, keys), bf),
                pltpu.VMEM((HEAD, keys), bf),
                pltpu.VMEM((tokens, pair), bf),
                pltpu.VMEM((tokens, pair), bf),
                pltpu.VMEM((tokens, pair), bf),
                pltpu.VMEM((keys, HEAD), f32),
                pltpu.VMEM((keys, HEAD), f32),
                pltpu.VMEM((slab, GROUP * BLOCK), f32),
                pltpu.VMEM((slab, GROUP * BLOCK), bf),
            ],
        ),
        out_shape=out_shape,
        compiler_params=pltpu.CompilerParams(vmem_limit_bytes=48 * 1024 * 1024),
        cost_estimate=HEAVY if chunk else LIGHT,
        name="attention",
    )(place, opened, lo, *own, near, *halo, *near_do, *far_do)


def body(queries, keys, values, grad_out, band_mask, segment_ids):
    n_ctx, n_mp = lax.axis_size("ctx"), lax.axis_size("mp")
    rows = queries.shape[0]
    piece = rows // n_mp
    heads_mp = KV_HEADS // n_mp
    heads_core = heads_mp // 2
    heads_chunk = heads_core // CHUNKS
    pair = GROUP * HEAD
    wide = heads_chunk * pair
    bf = jnp.bfloat16
    ctx, mp = lax.axis_index("ctx"), lax.axis_index("mp")
    core, chip = lax.rem(ctx, 2), ctx // 2
    place = jnp.stack([core, mp]).astype(jnp.int32)

    def send(x, target):
        return lax.ppermute(x, AXES, routes(target, n_ctx, n_mp))

    def half_at(side, first):
        return lambda g, sc: (0, (sc[0] if side == 0 else 1 - sc[0]) * heads_core + first + g)

    def local_at(g, sc):
        return (0, g)

    def pack_halo(first, after):
        sides = [
            [(x, (rows, HEAD), half_at(side, first)) for x in (keys, values)] for side in range(2)
        ]
        out = ((rows, wide), (rows, pair), local_at, 1)
        return pack(place, heads_chunk, sides, [out] * 2, after, "pack_halo")

    def grad_at(dm, side, first):
        def index(g, sc):
            core_to = sc[0] if side == 0 else 1 - sc[0]
            return (0, (lax.rem(sc[1] + dm, n_mp) * 2 + core_to) * heads_core + first + g)

        return index

    halos = [pack_halo(0, ())]
    (near_do,) = pack(
        place,
        heads_core,
        [
            [
                (
                    grad_out,
                    (piece, pair),
                    lambda g, sc, m=m: (0, (m * 2 + 1 - sc[0]) * heads_core + g),
                )
                for m in range(n_mp)
            ]
        ],
        [((rows, heads_core * pair), (rows, pair), local_at, 0)],
        halos[0],
        "pack_near_grad",
    )
    swap = lambda c, m: (c ^ 1, m)
    near_do = send(near_do, swap)
    (near,) = pack(
        place,
        heads_core,
        [
            [(queries, (rows, pair), half_at(1, 0))]
            + [(x, (rows, HEAD), half_at(1, 0)) for x in (keys, values)]
        ],
        [((rows, heads_core * 2 * pair), (rows, 2 * pair), local_at, 1)],
        halos[0],
        "pack_near",
    )
    near = send(near, swap)
    halo_in, far_do = [], []
    for i in range(CHUNKS):
        first = i * heads_chunk
        if i:
            halos.append(pack_halo(first, sent))
        halo_in.append(
            (
                send(halos[i][0], lambda c, m: (c + 2, m)),
                send(halos[i][1], lambda c, m: ((c + 2) ^ 1, m)),
            )
        )
        sent = pack(
            place,
            heads_chunk,
            [
                [
                    (grad_out, (piece, pair), grad_at(dm, 0, first)),
                    (
                        near_do,
                        (piece, pair),
                        lambda g, sc, dm=dm: (lax.rem(sc[1] + dm, n_mp), first + g),
                    ),
                ]
                for dm in range(1, n_mp)
            ],
            [((2 * piece, wide), (2 * piece, pair), local_at, 0)] * (n_mp - 1),
            halos[i] if i else (),
            "pack_far_grad",
        )
        far_do.append(
            [
                send(sent[dm - 1], lambda c, m: (c, (m + dm) % n_mp))
                for dm in range(1, n_mp)
            ]
        )

    tokens = 2 * rows
    padded = jnp.concatenate([jnp.full((WINDOW,), -1, jnp.int32), segment_ids])
    ids = lax.dynamic_slice_in_dim(padded, chip * tokens, WINDOW + tokens, 0)
    before = jnp.sum((ids[:, None] < ids[None, WINDOW:]).astype(jnp.int32), axis=0)
    lo = jnp.maximum(before, jnp.arange(1, tokens + 1, dtype=jnp.int32))[None, :]
    blocks = tokens // BLOCK
    opened = lax.dynamic_slice_in_dim(band_mask, chip * blocks, blocks, 0).reshape(-1)

    out_parts, dq_parts, across_parts, near_parts, far_parts = [], [], [], [], []
    for i in range(CHUNKS):
        dq_same, dkv_same, dh_same, dh_oth, across, o_own, *o_far = attention(
            n_mp,
            rows,
            i,
            heads_core,
            heads_chunk,
            place,
            opened,
            lo,
            (queries, keys, values),
            near,
            halo_in[i],
            (grad_out, near_do),
            far_do[i],
        )
        if i:
            earlier = (far_parts[-1], out_parts[-1], across_parts[-1])
            (dh_same, dh_oth, o_far, across), earlier = lax.optimization_barrier(
                ((dh_same, dh_oth, o_far, across), earlier)
            )
            far_parts[-1], out_parts[-1], across_parts[-1] = earlier
        far_parts.append(
            (
                send(dh_same, lambda c, m: (c - 2, m)),
                send(dh_oth, lambda c, m: ((c - 2) ^ 1 if c >= 2 else -1, m)),
            )
        )
        o_parts = [o_own]
        for dm in range(1, n_mp):
            o_parts.append(send(o_far[2 * dm - 2], lambda c, m: (c, (m + dm) % n_mp)))
            o_parts.append(send(o_far[2 * dm - 1], lambda c, m: (c ^ 1, (m + dm) % n_mp)))
        out_parts.append(o_parts)
        across_parts.append(send(across, swap))
        dq_parts.append(dq_same)
        near_parts.append(dkv_same)

    def out_column(chunk, dk, dm, g=0):
        def column(core, mp):
            core_from = core if dk == 0 else 1 - core
            mp_from = lax.rem(mp + n_mp - dm, n_mp)
            return ((mp_from * 2 + core_from) * heads_core + chunk * heads_chunk + g) * pair

        return column

    def query_column(chunk, side, g=0):
        def column(core, mp):
            half = core if side == 0 else 1 - core
            return (half * heads_core + chunk * heads_chunk + g) * pair

        return column

    arrays, jobs = [], []
    for i in range(CHUNKS):
        for at, part in enumerate(out_parts[i]):
            dk, dm = (at + 1) % 2 if at else 0, (at + 1) // 2
            jobs.append((len(arrays), 0, 0, 0, wide, out_column(i, dk, dm)))
            arrays.append(part)
        jobs.append((len(arrays), 0, 0, 1, wide, query_column(i, 0)))
        arrays.append(dq_parts[i])
        for g in range(heads_chunk):
            at = 3 * g * pair
            jobs.append((len(arrays), 0, at, 1, pair, query_column(i, 1, g)))
            jobs.append((len(arrays), piece, at + 2 * pair, 0, pair, out_column(i, 1, 0, g)))
        arrays.append(across_parts[i])
    attn_out, grad_queries = place_columns(
        place,
        arrays,
        [
            jax.ShapeDtypeStruct((piece, n_mp * heads_mp * pair), bf),
            jax.ShapeDtypeStruct(queries.shape, bf),
        ],
        jobs,
    )

    grads_kv = ()
    for i in range(CHUNKS):
        terms = (near_parts[i], far_parts[i][0], across_parts[i], far_parts[i][1])
        after = (attn_out,) if i == CHUNKS - 1 else ()
        grads_kv = sum_terms(place, i, heads_core, heads_chunk, terms, grads_kv, after)
    return attn_out, grad_queries, grads_kv[0], grads_kv[1]


def solution(mesh):
    placed = (P("ctx", "mp"), P("ctx", "mp"), P("ctx", "mp"), P(("ctx", "mp"), None), P(), P())
    return jax.shard_map(
        body,
        mesh=mesh,
        in_specs=placed,
        out_specs=(P(("ctx", "mp"), None), P("ctx", "mp"), P("ctx", "mp"), P("ctx", "mp")),
        check_vma=False,
    )
```

```python
import functools
import math

import jax
import jax.numpy as jnp
from jax import lax
from jax.experimental import pallas as pl
from jax.experimental.pallas import tpu as pltpu
from jax.sharding import PartitionSpec as P

KV_HEADS = 16
GROUP = 2
HEAD = 128
WINDOW = 1024
BLOCK = 128
SPAN = WINDOW // BLOCK + 1
CHUNKS = 2
ATTN_SCALE = 168.0 ** (-0.5)
EXP2_SCALE = ATTN_SCALE * math.log2(math.e)
MASKED = -1e30
FAR = 1 << 20
AXES = ("ctx", "mp")
NT = (((1,), (1,)), ((), ()))
NN = (((1,), (0,)), ((), ()))
LIGHT = pl.CostEstimate(flops=0, bytes_accessed=1024, transcendentals=0)
VMEM_LIMIT = 63 * 1024 * 1024
HEAVY = pl.CostEstimate(flops=25_000_000_000, bytes_accessed=1024, transcendentals=0)


def dot(a, b, dims=NN):
    return lax.dot_general(a, b, dims, preferred_element_type=jnp.float32)


def routes(target, n_ctx, n_mp):
    out = []
    for c in range(n_ctx):
        for m in range(n_mp):
            d = target(c, m)
            if 0 <= d[0] < n_ctx:
                out.append((c * n_mp + m, d[0] * n_mp + d[1]))
    return out


def gather_kernel(plan, n_in, shapes, sc_ref, *refs):
    n = len(shapes)
    outs, images, sems = refs[n_in : n_in + n], refs[n_in + n : n_in + 2 * n], refs[-2:]
    into = [[] for _ in shapes]
    count = 0
    for src, dst, src_at, dst_at, size in plan(sc_ref[0], sc_ref[1]):
        copy = pltpu.make_async_copy(
            refs[src].at[tuple(pl.ds(at, by) for at, by in zip(src_at, size))],
            images[dst].at[tuple(pl.ds(at, by) for at, by in zip(dst_at, size))],
            sems[0].at[count],
        )
        copy.start()
        into[dst].append(copy)
        count += 1
    written = []
    for dst in range(n):
        for copy in into[dst]:
            copy.wait()
        written.append(pltpu.make_async_copy(images[dst], outs[dst], sems[1].at[dst]))
        written[-1].start()
    for copy in written:
        copy.wait()


def gather(plan, count, place, arrays, shapes, cost, after=(), name="gather"):
    hbm = pl.BlockSpec(memory_space=pl.ANY)
    return pl.pallas_call(
        functools.partial(gather_kernel, plan, len(arrays) + len(after), shapes),
        in_specs=[pl.BlockSpec(memory_space=pltpu.SMEM)] + [hbm] * (len(arrays) + len(after)),
        out_specs=[hbm] * len(shapes),
        out_shape=[jax.ShapeDtypeStruct(shape, jnp.bfloat16) for shape in shapes],
        scratch_shapes=[pltpu.VMEM(shape, jnp.bfloat16) for shape in shapes]
        + [pltpu.SemaphoreType.DMA((count,)), pltpu.SemaphoreType.DMA((len(shapes),))],
        compiler_params=pltpu.CompilerParams(vmem_limit_bytes=VMEM_LIMIT),
        cost_estimate=cost,
        name=name,
    )(place, *arrays, *after)


def attention_kernel(n_mp, rows, sc_ref, open_ref, lo_ref, *refs):
    q_own, k_own, v_own, q_near, k_near, v_near = refs[:6]
    kh_same, vh_same, kh_oth, vh_oth, do_own, do_oth = refs[6:12]
    do_far = refs[12 : 10 + 2 * n_mp]
    refs = refs[10 + 2 * n_mp :]
    dq_same, dkv_same, dh_same, dh_oth, across, o_own = refs[:6]
    o_far = refs[6 : 4 + 2 * n_mp]
    qs, ks, vs, k_t, v_t, dos, os, dqs, dk, dv = refs[4 + 2 * n_mp : 14 + 2 * n_mp]
    s_refs, e_refs, ds_refs = refs[-6:-4], refs[-4:-2], refs[-2:]
    core, mp = sc_ref[0], sc_ref[1]
    piece, pair = rows // n_mp, GROUP * HEAD
    same = pl.ds(pl.multiple_of(core * rows, rows), rows)
    oth = pl.ds(pl.multiple_of((1 - core) * rows, rows), rows)
    same_kv = pl.ds(pl.multiple_of(WINDOW + core * rows, rows), rows)
    oth_kv = pl.ds(pl.multiple_of(WINDOW + (1 - core) * rows, rows), rows)

    def piece_at(dk_, dm):
        k_at = core if dk_ == 0 else 1 - core
        return pl.ds(pl.multiple_of(k_at * rows + lax.rem(mp + dm, n_mp) * piece, piece), piece)

    qs[same, :] = q_own[...]
    qs[oth, :] = q_near[...]
    ks[same, :] = kh_same[...]
    ks[oth, :] = kh_oth[...]
    ks[same_kv, :] = k_own[...]
    ks[oth_kv, :] = k_near[...]
    vs[same, :] = vh_same[...]
    vs[oth, :] = vh_oth[...]
    vs[same_kv, :] = v_own[...]
    vs[oth_kv, :] = v_near[...]
    dos[piece_at(0, 0), :] = do_own[...]
    dos[piece_at(1, 0), :] = do_oth[...]
    for at in range(n_mp - 1):
        dos[piece_at(0, n_mp - 1 - at), :] = do_far[2 * at][...]
        dos[piece_at(1, n_mp - 1 - at), :] = do_far[2 * at + 1][...]
    dk[...] = jnp.zeros_like(dk)
    dv[...] = jnp.zeros_like(dv)
    for t in range(ks.shape[0] // 256):
        at = slice(t * 256, t * 256 + 256)
        k_t[:, at] = ks[at, :].T
        v_t[:, at] = vs[at, :].T

    width = GROUP * BLOCK
    row = lax.broadcasted_iota(jnp.int32, (BLOCK, width), 0)
    lane = lax.broadcasted_iota(jnp.int32, (BLOCK, width), 1)
    causal = row <= lax.rem(lane, BLOCK)

    def by_rows(x, reduce):
        return reduce(x.reshape(BLOCK // 8, 8, width), axis=0)

    def forward(b):
        s_ref, e_ref = s_refs[b % 2], e_refs[b % 2]
        at_q = slice(b * BLOCK, b * BLOCK + BLOCK)
        q_blk = jnp.concatenate([qs[at_q, :HEAD], qs[at_q, HEAD:]], axis=0)
        lo = jnp.concatenate([lo_ref[:, at_q]] * GROUP, axis=1)
        top = jnp.full((8, width), MASKED, jnp.float32)
        for j in range(SPAN):
            part = slice(j * BLOCK, j * BLOCK + BLOCK)
            s = dot(ks[(b + j) * BLOCK : (b + j + 1) * BLOCK, :], q_blk, NT)
            closed = jnp.where(open_ref[b * SPAN + SPAN - 1 - j] == 1, 0, FAR)
            valid = row >= jnp.maximum(lo - (b + j) * BLOCK, closed)
            if j == SPAN - 1:
                valid = valid & causal
            s = jnp.where(valid, s, MASKED)
            s_ref[part, :] = s
            top = jnp.maximum(top, by_rows(s, jnp.max))
        top = jnp.max(top, axis=0, keepdims=True)
        total = jnp.zeros((8, width), jnp.float32)
        for j in range(SPAN):
            part = slice(j * BLOCK, j * BLOCK + BLOCK)
            e = jnp.exp2((s_ref[part, :] - top) * EXP2_SCALE)
            total = total + by_rows(e, jnp.sum)
            e_ref[part, :] = e.astype(jnp.bfloat16)
        return q_blk, 1.0 / jnp.sum(total, axis=0, keepdims=True)

    def backward(b, q_blk, inverse):
        e_ref, ds_ref = e_refs[b % 2], ds_refs[b % 2]
        at_q = slice(b * BLOCK, b * BLOCK + BLOCK)
        at_keys = slice(b * BLOCK, (b + SPAN) * BLOCK)
        o_t = (dot(v_t[:, at_keys], e_ref[...]) * inverse).astype(jnp.bfloat16)
        os[at_q, :HEAD] = o_t[:, :BLOCK].T
        os[at_q, HEAD:] = o_t[:, BLOCK:].T
        do_t = jnp.concatenate([dos[at_q, :HEAD].T, dos[at_q, HEAD:].T], axis=1)
        do_t = (do_t.astype(jnp.float32) * inverse).astype(jnp.bfloat16)
        delta = jnp.sum(
            do_t.astype(jnp.float32) * o_t.astype(jnp.float32), axis=0, keepdims=True
        )
        for j in range(SPAN):
            part = slice(j * BLOCK, j * BLOCK + BLOCK)
            dp = dot(vs[(b + j) * BLOCK : (b + j + 1) * BLOCK, :], do_t)
            ds_ref[part, :] = (e_ref[part, :].astype(jnp.float32) * (dp - delta)).astype(
                jnp.bfloat16
            )
        dv[at_keys, :] += dot(e_ref[...], do_t, NT)
        dk[at_keys, :] += dot(ds_ref[...], q_blk)
        dq_t = (dot(k_t[:, at_keys], ds_ref[...]) * ATTN_SCALE).astype(jnp.bfloat16)
        dqs[at_q, :HEAD] = dq_t[:, :BLOCK].T
        dqs[at_q, HEAD:] = dq_t[:, BLOCK:].T

    blocks = qs.shape[0] // BLOCK
    ahead = forward(0)
    for b in range(blocks):
        now, ahead = ahead, forward(b + 1) if b + 1 < blocks else None
        backward(b, *now)

    dq_same[...] = dqs[same, :]
    wide = across.shape[1] // 3
    at_g = pl.multiple_of(pl.program_id(0) * pair, pair)
    across[:, pl.ds(at_g, pair)] = dqs[oth, :]
    across[:, pl.ds(2 * wide + at_g, pair)] = os[oth, :]
    o_own[...] = os[piece_at(0, 0), :]
    for at in range(n_mp - 1):
        o_far[2 * at][...] = os[piece_at(0, at + 1), :]
        o_far[2 * at + 1][...] = os[piece_at(1, at + 1), :]
    for out, at in ((dkv_same, same_kv), (dh_same, same), (dh_oth, oth)):
        out[:, :HEAD] = (dk[at, :] * ATTN_SCALE).astype(out.dtype)
        out[:, HEAD:] = dv[at, :].astype(out.dtype)
    across[:, pl.ds(wide + at_g, HEAD)] = (dk[oth_kv, :] * ATTN_SCALE).astype(across.dtype)
    across[:, pl.ds(wide + at_g + HEAD, HEAD)] = dv[oth_kv, :].astype(across.dtype)


def attention(n_mp, rows, chunk, heads, place, opened, lo, own, near, halo, grad_out, far_do):
    heads_mp = 2 * CHUNKS * heads
    piece, pair = rows // n_mp, GROUP * HEAD
    heads_chunk, first = heads, chunk * heads

    def at_head(g, sc, *unused):
        return (0, 2 * first + sc[0] * heads + g)

    def at_grad(g, sc, *unused):
        return (0, sc[1] * heads_mp + 2 * first + sc[0] * heads + g)

    def at_near(column):
        return lambda g, *unused: (0, column + first + g)

    def at_near_do(g, *unused):
        return (chunk, CHUNKS * 2 * heads + g)

    def at_halo(which):
        return lambda g, sc, *unused: (0, which * 2 * heads + sc[0] * heads + g)

    def at_local(g, *unused):
        return (0, g)

    in_specs = [pl.BlockSpec((1, 2 * rows), lambda g, *unused: (0, 0))]
    in_specs += [pl.BlockSpec((rows, pair), at_head)]
    in_specs += [pl.BlockSpec((rows, HEAD), at_head)] * 2
    in_specs += [pl.BlockSpec((rows, pair), at_near(0))]
    in_specs += [pl.BlockSpec((rows, HEAD), at_near(n * CHUNKS * heads)) for n in (2, 3)]
    in_specs += [pl.BlockSpec((rows, HEAD), at_halo(n)) for n in (0, 1, 0, 1)]
    in_specs += [pl.BlockSpec((piece, pair), at_grad), pl.BlockSpec((piece, pair), at_near_do)]
    in_specs += [pl.BlockSpec((piece, pair), at_local)] * (2 * n_mp - 2)
    wide = heads_chunk * pair
    bf, f32 = jnp.bfloat16, jnp.float32
    out_specs = [pl.BlockSpec((rows, pair), at_local)] * 4
    out_specs += [pl.BlockSpec((rows, 3 * wide), lambda g, *unused: (0, 0))]
    out_specs += [pl.BlockSpec((piece, pair), at_local)] * (2 * n_mp - 1)
    out_shape = [jax.ShapeDtypeStruct((rows, wide), t) for t in (bf, bf, bf, bf)]
    out_shape += [jax.ShapeDtypeStruct((rows, 3 * wide), bf)]
    out_shape += [jax.ShapeDtypeStruct((piece, wide), bf)] * (2 * n_mp - 1)
    tokens, keys, slab = 2 * rows, WINDOW + 2 * rows, SPAN * BLOCK
    return pl.pallas_call(
        functools.partial(attention_kernel, n_mp, rows),
        grid_spec=pltpu.PrefetchScalarGridSpec(
            num_scalar_prefetch=2,
            grid=(heads_chunk,),
            in_specs=in_specs,
            out_specs=out_specs,
            scratch_shapes=[
                pltpu.VMEM((tokens, pair), bf),
                pltpu.VMEM((keys, HEAD), bf),
                pltpu.VMEM((keys, HEAD), bf),
                pltpu.VMEM((HEAD, keys), bf),
                pltpu.VMEM((HEAD, keys), bf),
                pltpu.VMEM((tokens, pair), bf),
                pltpu.VMEM((tokens, pair), bf),
                pltpu.VMEM((tokens, pair), bf),
                pltpu.VMEM((keys, HEAD), f32),
                pltpu.VMEM((keys, HEAD), f32),
            ]
            + [pltpu.VMEM((slab, GROUP * BLOCK), t) for t in (f32, f32, bf, bf, bf, bf)],
        ),
        out_shape=out_shape,
        compiler_params=pltpu.CompilerParams(vmem_limit_bytes=VMEM_LIMIT),
        cost_estimate=HEAVY if chunk else LIGHT,
        name="attention",
    )(place, opened, lo, *own, near, near, near, halo[0], halo[0], halo[1], halo[1], grad_out, near, *far_do)


def sum_kernel(heads, sc_ref, near_same, far_same, near_oth, far_oth, *refs):
    dk, dv = refs[-2:]

    def add(near, far):
        for g in range(heads):
            at = 2 * g * HEAD
            to = slice(g * HEAD, g * HEAD + HEAD)
            for out, col in ((dk, at), (dv, at + HEAD)):
                terms = [x[:, col : col + HEAD].astype(jnp.float32) for x in (near, far)]
                out[:, to] = (terms[0] + terms[1]).astype(out.dtype)

    @pl.when(pl.program_id(0) == 0)
    def _():
        add(near_same, far_same)

    @pl.when(pl.program_id(0) == 1)
    def _():
        add(near_oth, far_oth)


def sum_terms(place, chunk, heads, n_heads, terms, before, after=()):
    rows, wide = terms[0].shape

    def at_first(side, sc):
        return (0, 0)

    def at_across(side, sc):
        return (0, 1)

    def at_out(side, sc):
        return (0, 2 * chunk + jnp.where(side == 0, sc[0], 1 - sc[0]))

    shape = jax.ShapeDtypeStruct((rows, n_heads * HEAD), jnp.bfloat16)
    in_specs = [pl.BlockSpec((rows, wide), at) for at in (at_first, at_first, at_across, at_first)]
    return pl.pallas_call(
        functools.partial(sum_kernel, heads),
        grid_spec=pltpu.PrefetchScalarGridSpec(
            num_scalar_prefetch=1,
            grid=(2,),
            in_specs=in_specs + [pl.BlockSpec(memory_space=pl.ANY)] * len((*before, *after)),
            out_specs=[pl.BlockSpec((rows, heads * HEAD), at_out)] * 2,
        ),
        out_shape=[shape, shape],
        input_output_aliases={5: 0, 6: 1} if before else {},
        compiler_params=pltpu.CompilerParams(vmem_limit_bytes=VMEM_LIMIT),
        cost_estimate=LIGHT,
        name="sum_terms",
    )(place, *terms, *before, *after)


def body(queries, keys, values, grad_out, band_mask, segment_ids):
    n_ctx, n_mp = lax.axis_size("ctx"), lax.axis_size("mp")
    rows = queries.shape[0]
    piece = rows // n_mp
    heads_mp = KV_HEADS // n_mp
    heads = heads_mp // (2 * CHUNKS)
    pair = GROUP * HEAD
    wide = heads * pair
    bf = jnp.bfloat16
    ctx, mp = lax.axis_index("ctx"), lax.axis_index("mp")
    core, chip = lax.rem(ctx, 2), ctx // 2
    place = jnp.stack([core, mp]).astype(jnp.int32)

    def send(x, target):
        return lax.ppermute(x, AXES, routes(target, n_ctx, n_mp))

    swap = lambda c, m: (c ^ 1, m)

    def first_head(chunk, core):
        return (2 * chunk + core) * heads

    def col(head, width):
        return pl.multiple_of(head * width, HEAD)

    def plan_halo(chunk):
        def plan(core, mp):
            at, by = first_head(chunk, 0) * HEAD, 2 * heads * HEAD
            return [(n, 0, (0, at), (0, n * by), (rows, by)) for n in range(2)]

        return plan

    def pack_halo(chunk, after):
        shape = (rows, 4 * heads * HEAD)
        (packed,) = gather(
            plan_halo(chunk), 2, place, (keys, values), [shape], HEAVY, after, "pack_halo"
        )
        return packed

    far = [(dk, dm) for dm in range(1, n_mp) for dk in range(2)]
    n_far = len(far)

    def plan_near(core, mp):
        jobs = []
        for at, (dk, dm) in enumerate(far):
            mp_to, core_to = lax.rem(mp + dm, n_mp), core if dk == 0 else 1 - core
            for i in range(CHUNKS):
                src = col(mp_to * heads_mp + first_head(i, core_to), pair)
                jobs.append((3, i * n_far + at, (0, src), (0, 0), (piece, wide)))
        for n, width, to in ((0, pair, 0), (1, HEAD, CHUNKS * wide), (2, HEAD, 3 * CHUNKS * wide // 2)):
            for i in range(CHUNKS):
                src = col(first_head(i, 1 - core), width)
                by = heads * width
                jobs.append((n, CHUNKS * n_far, (0, src), (0, to + i * by), (rows, by)))
        for i in range(CHUNKS):
            src = col(mp * heads_mp + first_head(i, 1 - core), pair)
            jobs.append((3, CHUNKS * n_far, (0, src), (i * piece, 2 * CHUNKS * wide), (piece, wide)))
        return jobs

    halo = pack_halo(0, ())
    *far_do, near = gather(
        plan_near,
        CHUNKS * (n_far + 4),
        place,
        (queries, keys, values, grad_out),
        [(piece, wide)] * (CHUNKS * n_far) + [(rows, (2 * CHUNKS + 1) * wide)],
        HEAVY,
        (halo,),
        "pack_near",
    )
    far_do = [
        [
            send(x, lambda c, m: (c ^ dk, (m + dm) % n_mp))
            for x, (dk, dm) in zip(far_do[i * n_far : (i + 1) * n_far], far)
        ]
        for i in range(CHUNKS)
    ]
    halos = [halo] + [pack_halo(i, (near,)) for i in range(1, CHUNKS)]
    halo_in = [send(halo, lambda c, m: (c + 2, m)) for halo in halos]
    near = send(near, swap)

    tokens = 2 * rows
    padded = jnp.concatenate([jnp.full((WINDOW,), -1, jnp.int32), segment_ids])
    ids = lax.dynamic_slice_in_dim(padded, chip * tokens, WINDOW + tokens, 0)
    before = jnp.sum((ids[:, None] < ids[None, WINDOW:]).astype(jnp.int32), axis=0)
    lo = jnp.maximum(before, jnp.arange(1, tokens + 1, dtype=jnp.int32))[None, :]
    blocks = tokens // BLOCK
    opened = lax.dynamic_slice_in_dim(band_mask, chip * blocks, blocks, 0).reshape(-1)

    out_parts, dq_parts, across_parts, near_parts, far_parts = [], [], [], [], []
    for i in range(CHUNKS):
        ahead = halos[i + 1 :]
        halo, far_do[i], dq_parts, ahead, lo, opened = lax.optimization_barrier(
            (halo_in[i], far_do[i], dq_parts, ahead, lo, opened)
        )
        halo = (halo, send(halo, swap))
        dq_same, dkv_same, dh_same, dh_oth, across, o_own, *o_far = attention(
            n_mp,
            rows,
            i,
            heads,
            place,
            opened,
            lo,
            (queries, keys, values),
            near,
            halo,
            grad_out,
            far_do[i],
        )
        if i:
            earlier = (far_parts[-1], out_parts[-1], across_parts[-1])
            (dh_same, dh_oth, o_far, across), earlier = lax.optimization_barrier(
                ((dh_same, dh_oth, o_far, across), earlier)
            )
            far_parts[-1], out_parts[-1], across_parts[-1] = earlier
        far_parts.append(
            (
                send(dh_same, lambda c, m: (c - 2, m)),
                send(dh_oth, lambda c, m: ((c - 2) ^ 1 if c >= 2 else -1, m)),
            )
        )
        o_parts = [o_own]
        for dm in range(1, n_mp):
            o_parts.append(send(o_far[2 * dm - 2], lambda c, m: (c, (m + dm) % n_mp)))
            o_parts.append(send(o_far[2 * dm - 1], lambda c, m: (c ^ 1, (m + dm) % n_mp)))
        out_parts.append(o_parts)
        across_parts.append(send(across, swap))
        dq_parts.append(dq_same)
        near_parts.append(dkv_same)

    arrays = [
        x for o, a, q in zip(out_parts, across_parts, dq_parts) for x in (*o, a, q)
    ]

    def plan_out(core, mp):
        jobs, at = [], 0
        for i in range(CHUNKS):
            for dk, dm in [(0, 0)] + far:
                mp_from, core_from = lax.rem(mp + n_mp - dm, n_mp), core if dk == 0 else 1 - core
                to = col(mp_from * heads_mp + first_head(i, core_from), pair)
                jobs.append((at, 0, (0, 0), (0, to), (piece, wide)))
                at += 1
            to = col(mp * heads_mp + first_head(i, 1 - core), pair)
            rows_at = pl.multiple_of(mp * piece, piece)
            jobs.append((at, 0, (rows_at, 2 * wide), (0, to), (piece, wide)))
            to = col(first_head(i, 1 - core), pair)
            jobs.append((at, 1, (0, 0), (0, to), (rows, wide)))
            to = col(first_head(i, core), pair)
            jobs.append((at + 1, 1, (0, 0), (0, to), (rows, wide)))
            at += 2
        return jobs

    attn_out, grad_queries = gather(
        plan_out,
        CHUNKS * (n_far + 4),
        place,
        arrays,
        [(piece, n_mp * heads_mp * pair), (rows, heads_mp * pair)],
        LIGHT,
        (),
        "put_together",
    )

    grads_kv = ()
    for i in range(CHUNKS):
        terms = (near_parts[i], far_parts[i][0], across_parts[i], far_parts[i][1])
        after = (attn_out,) if i == CHUNKS - 1 else ()
        grads_kv = sum_terms(place, i, heads, heads_mp, terms, grads_kv, after)
    return attn_out, grad_queries, grads_kv[0], grads_kv[1]


def solution(mesh):
    placed = (P("ctx", "mp"), P("ctx", "mp"), P("ctx", "mp"), P(("ctx", "mp"), None), P(), P())
    return jax.shard_map(
        body,
        mesh=mesh,
        in_specs=placed,
        out_specs=(P(("ctx", "mp"), None), P("ctx", "mp"), P("ctx", "mp"), P("ctx", "mp")),
        check_vma=False,
    )
```

```python
import functools
import math

import jax
import jax.numpy as jnp
from jax import lax
from jax.experimental import pallas as pl
from jax.experimental.pallas import tpu as pltpu
from jax.sharding import PartitionSpec as P

KV_HEADS = 16
GROUP = 2
HEAD = 128
WINDOW = 1024
BLOCK = 128
SPAN = WINDOW // BLOCK + 1
CHUNKS = 2
ATTN_SCALE = 168.0 ** (-0.5)
EXP2_SCALE = ATTN_SCALE * math.log2(math.e)
MASKED = -1e30
FAR = 1 << 20
AXES = ("ctx", "mp")
NT = (((1,), (1,)), ((), ()))
NN = (((1,), (0,)), ((), ()))
LIGHT = pl.CostEstimate(flops=0, bytes_accessed=1024, transcendentals=0)
VMEM_LIMIT = (64 * 1024 - 128) * 1024
HEAVY = pl.CostEstimate(flops=25_000_000_000, bytes_accessed=1024, transcendentals=0)


def dot(a, b, dims=NN):
    return lax.dot_general(a, b, dims, preferred_element_type=jnp.float32)


def routes(target, n_ctx, n_mp):
    out = []
    for c in range(n_ctx):
        for m in range(n_mp):
            d = target(c, m)
            if 0 <= d[0] < n_ctx:
                out.append((c * n_mp + m, d[0] * n_mp + d[1]))
    return out


def gather_kernel(plan, n_in, shapes, sc_ref, *refs):
    n = len(shapes)
    outs, images, sems = refs[n_in : n_in + n], refs[n_in + n : n_in + 2 * n], refs[-2:]
    into = [[] for _ in shapes]
    count = 0
    for src, dst, src_at, dst_at, size in plan(sc_ref[0], sc_ref[1]):
        copy = pltpu.make_async_copy(
            refs[src].at[tuple(pl.ds(at, by) for at, by in zip(src_at, size))],
            images[dst].at[tuple(pl.ds(at, by) for at, by in zip(dst_at, size))],
            sems[0].at[count],
        )
        copy.start()
        into[dst].append(copy)
        count += 1
    written = []
    for dst in range(n):
        for copy in into[dst]:
            copy.wait()
        written.append(pltpu.make_async_copy(images[dst], outs[dst], sems[1].at[dst]))
        written[-1].start()
    for copy in written:
        copy.wait()


def gather(plan, count, place, arrays, shapes, cost, after=(), name="gather"):
    hbm = pl.BlockSpec(memory_space=pl.ANY)
    return pl.pallas_call(
        functools.partial(gather_kernel, plan, len(arrays) + len(after), shapes),
        in_specs=[pl.BlockSpec(memory_space=pltpu.SMEM)] + [hbm] * (len(arrays) + len(after)),
        out_specs=[hbm] * len(shapes),
        out_shape=[jax.ShapeDtypeStruct(shape, jnp.bfloat16) for shape in shapes],
        scratch_shapes=[pltpu.VMEM(shape, jnp.bfloat16) for shape in shapes]
        + [pltpu.SemaphoreType.DMA((count,)), pltpu.SemaphoreType.DMA((len(shapes),))],
        compiler_params=pltpu.CompilerParams(vmem_limit_bytes=VMEM_LIMIT),
        cost_estimate=cost,
        name=name,
    )(place, *arrays, *after)


def attention_kernel(n_mp, rows, whole, sc_ref, open_ref, lo_ref, *refs):
    q_own, k_own, v_own, q_near, k_near, v_near = refs[:6]
    kh_same, vh_same, kh_oth, vh_oth, do_own, do_oth = refs[6:12]
    do_far = refs[12 : 10 + 2 * n_mp]
    refs = refs[10 + 2 * n_mp :]
    n_back = 1 if whole else 2
    dq_same, dkv_same, across, o_own, *o_far = refs[: 2 + 2 * n_mp]
    back = refs[2 + 2 * n_mp : 2 + 2 * n_mp + n_back]
    refs = refs[2 + 2 * n_mp + n_back :]
    qs, ks, vs, k_t, v_t, dos, os, dqs, dk, dv = refs[:10]
    s_refs, e_refs, ds_refs = refs[-6:-4], refs[-4:-2], refs[-2:]
    core, mp = sc_ref[0], sc_ref[1]
    piece, pair = rows // n_mp, GROUP * HEAD
    same = pl.ds(pl.multiple_of(core * rows, rows), rows)
    oth = pl.ds(pl.multiple_of((1 - core) * rows, rows), rows)
    same_kv = pl.ds(pl.multiple_of(WINDOW + core * rows, rows), rows)
    oth_kv = pl.ds(pl.multiple_of(WINDOW + (1 - core) * rows, rows), rows)

    def piece_at(dk_, dm):
        k_at = core if dk_ == 0 else 1 - core
        return pl.ds(pl.multiple_of(k_at * rows + lax.rem(mp + dm, n_mp) * piece, piece), piece)

    qs[same, :] = q_own[...]
    qs[oth, :] = q_near[...]
    ks[same, :] = kh_same[...]
    ks[oth, :] = kh_oth[...]
    ks[same_kv, :] = k_own[...]
    ks[oth_kv, :] = k_near[...]
    vs[same, :] = vh_same[...]
    vs[oth, :] = vh_oth[...]
    vs[same_kv, :] = v_own[...]
    vs[oth_kv, :] = v_near[...]
    dos[piece_at(0, 0), :] = do_own[...]
    dos[piece_at(1, 0), :] = do_oth[...]
    for at in range(n_mp - 1):
        dos[piece_at(0, n_mp - 1 - at), :] = do_far[2 * at][...]
        dos[piece_at(1, n_mp - 1 - at), :] = do_far[2 * at + 1][...]
    dk[...] = jnp.zeros_like(dk)
    dv[...] = jnp.zeros_like(dv)
    for t in range(ks.shape[0] // 256):
        at = slice(t * 256, t * 256 + 256)
        k_t[:, at] = ks[at, :].T
        v_t[:, at] = vs[at, :].T

    width = GROUP * BLOCK
    row = lax.broadcasted_iota(jnp.int32, (BLOCK, width), 0)
    lane = lax.broadcasted_iota(jnp.int32, (BLOCK, width), 1)
    causal = row <= lax.rem(lane, BLOCK)

    def by_rows(x, reduce):
        return reduce(x.reshape(BLOCK // 8, 8, width), axis=0)

    def forward(b):
        s_ref, e_ref = s_refs[b % 2], e_refs[b % 2]
        at_q = slice(b * BLOCK, b * BLOCK + BLOCK)
        q_blk = jnp.concatenate([qs[at_q, :HEAD], qs[at_q, HEAD:]], axis=0)
        lo = jnp.concatenate([lo_ref[:, at_q]] * GROUP, axis=1)
        top = jnp.full((8, width), MASKED, jnp.float32)
        for j in range(SPAN):
            part = slice(j * BLOCK, j * BLOCK + BLOCK)
            s = dot(ks[(b + j) * BLOCK : (b + j + 1) * BLOCK, :], q_blk, NT)
            closed = jnp.where(open_ref[b * SPAN + SPAN - 1 - j] == 1, 0, FAR)
            valid = row >= jnp.maximum(lo - (b + j) * BLOCK, closed)
            if j == SPAN - 1:
                valid = valid & causal
            s = jnp.where(valid, s, MASKED)
            s_ref[part, :] = s
            top = jnp.maximum(top, by_rows(s, jnp.max))
        top = jnp.max(top, axis=0, keepdims=True)
        total = jnp.zeros((8, width), jnp.float32)
        for j in range(SPAN):
            part = slice(j * BLOCK, j * BLOCK + BLOCK)
            e = jnp.exp2((s_ref[part, :] - top) * EXP2_SCALE)
            total = total + by_rows(e, jnp.sum)
            e_ref[part, :] = e.astype(jnp.bfloat16)
        return q_blk, 1.0 / jnp.sum(total, axis=0, keepdims=True)

    def backward(b, q_blk, inverse):
        e_ref, ds_ref = e_refs[b % 2], ds_refs[b % 2]
        at_q = slice(b * BLOCK, b * BLOCK + BLOCK)
        at_keys = slice(b * BLOCK, (b + SPAN) * BLOCK)
        o_t = (dot(v_t[:, at_keys], e_ref[...]) * inverse).astype(jnp.bfloat16)
        os[at_q, :HEAD] = o_t[:, :BLOCK].T
        os[at_q, HEAD:] = o_t[:, BLOCK:].T
        do_t = jnp.concatenate([dos[at_q, :HEAD].T, dos[at_q, HEAD:].T], axis=1)
        do_t = (do_t.astype(jnp.float32) * inverse).astype(jnp.bfloat16)
        delta = jnp.sum(
            do_t.astype(jnp.float32) * o_t.astype(jnp.float32), axis=0, keepdims=True
        )
        for j in range(SPAN):
            part = slice(j * BLOCK, j * BLOCK + BLOCK)
            dp = dot(vs[(b + j) * BLOCK : (b + j + 1) * BLOCK, :], do_t)
            ds_ref[part, :] = (e_ref[part, :].astype(jnp.float32) * (dp - delta)).astype(
                jnp.bfloat16
            )
        dv[at_keys, :] += dot(e_ref[...], do_t, NT)
        dk[at_keys, :] += dot(ds_ref[...], q_blk)
        dq_t = (dot(k_t[:, at_keys], ds_ref[...]) * ATTN_SCALE).astype(jnp.bfloat16)
        dqs[at_q, :HEAD] = dq_t[:, :BLOCK].T
        dqs[at_q, HEAD:] = dq_t[:, BLOCK:].T

    blocks = qs.shape[0] // BLOCK
    ahead = forward(0)
    for b in range(blocks):
        now, ahead = ahead, forward(b + 1) if b + 1 < blocks else None
        backward(b, *now)

    dq_same[...] = dqs[same, :]
    wide = across.shape[1] // 3
    at_g = pl.multiple_of(pl.program_id(0) * pair, pair)
    across[:, pl.ds(at_g, pair)] = dqs[oth, :]
    across[:, pl.ds(2 * wide + at_g, pair)] = os[oth, :]
    o_own[...] = os[piece_at(0, 0), :]
    for at in range(n_mp - 1):
        o_far[2 * at][...] = os[piece_at(0, at + 1), :]
        o_far[2 * at + 1][...] = os[piece_at(1, at + 1), :]
    ats = (slice(0, 2 * rows),) if whole else (same, oth)
    for out, at in ((dkv_same, same_kv), *zip(back, ats)):
        out[:, :HEAD] = (dk[at, :] * ATTN_SCALE).astype(out.dtype)
        out[:, HEAD:] = dv[at, :].astype(out.dtype)
    across[:, pl.ds(wide + at_g, HEAD)] = (dk[oth_kv, :] * ATTN_SCALE).astype(across.dtype)
    across[:, pl.ds(wide + at_g + HEAD, HEAD)] = dv[oth_kv, :].astype(across.dtype)


def attention(n_mp, rows, whole, chunk, heads, place, opened, lo, own, near, halo, grad_out, far_do):
    heads_mp = 2 * CHUNKS * heads
    piece, pair = rows // n_mp, GROUP * HEAD
    heads_chunk, first = heads, chunk * heads

    def at_head(g, sc, *unused):
        return (0, 2 * first + sc[0] * heads + g)

    def at_grad(g, sc, *unused):
        return (0, sc[1] * heads_mp + 2 * first + sc[0] * heads + g)

    def at_near(column):
        return lambda g, *unused: (0, column + first + g)

    def at_near_do(g, *unused):
        return (chunk, CHUNKS * 2 * heads + g)

    def at_halo(which, side):
        skip = 2 * heads if side and chunk else 0
        return lambda g, *unused: (0, skip + which * heads + g)

    def at_local(g, *unused):
        return (0, g)

    def at_handed(g, *unused):
        return (0, heads + g)

    in_specs = [pl.BlockSpec((1, 2 * rows), lambda g, *unused: (0, 0))]
    in_specs += [pl.BlockSpec((rows, pair), at_head)]
    in_specs += [pl.BlockSpec((rows, HEAD), at_head)] * 2
    in_specs += [pl.BlockSpec((rows, pair), at_near(0))]
    in_specs += [pl.BlockSpec((rows, HEAD), at_near(n * CHUNKS * heads)) for n in (2, 3)]
    in_specs += [pl.BlockSpec((rows, HEAD), at_halo(n % 2, n // 2)) for n in range(4)]
    in_specs += [pl.BlockSpec((piece, pair), at_grad), pl.BlockSpec((piece, pair), at_near_do)]
    in_specs += [pl.BlockSpec((piece, pair), at) for at in (at_local, at_handed)] * (n_mp - 1)
    wide = heads_chunk * pair
    bf, f32 = jnp.bfloat16, jnp.float32
    out_specs = [pl.BlockSpec((rows, pair), at_local)] * 2
    out_specs += [pl.BlockSpec((rows, 3 * wide), lambda g, *unused: (0, 0))]
    out_specs += [pl.BlockSpec((piece, pair), at_local)] * (2 * n_mp - 1)
    out_shape = [jax.ShapeDtypeStruct((rows, wide), bf)] * 2
    out_shape += [jax.ShapeDtypeStruct((rows, 3 * wide), bf)]
    out_shape += [jax.ShapeDtypeStruct((piece, wide), bf)] * (2 * n_mp - 1)
    n_back, rows_back = (1, 2 * rows) if whole else (2, rows)
    out_specs += [pl.BlockSpec((rows_back, pair), at_local)] * n_back
    out_shape += [jax.ShapeDtypeStruct((rows_back, wide), bf)] * n_back
    tokens, keys, slab = 2 * rows, WINDOW + 2 * rows, SPAN * BLOCK
    return pl.pallas_call(
        functools.partial(attention_kernel, n_mp, rows, whole),
        grid_spec=pltpu.PrefetchScalarGridSpec(
            num_scalar_prefetch=2,
            grid=(heads_chunk,),
            in_specs=in_specs,
            out_specs=out_specs,
            scratch_shapes=[
                pltpu.VMEM((tokens, pair), bf),
                pltpu.VMEM((keys, HEAD), bf),
                pltpu.VMEM((keys, HEAD), bf),
                pltpu.VMEM((HEAD, keys), bf),
                pltpu.VMEM((HEAD, keys), bf),
                pltpu.VMEM((tokens, pair), bf),
                pltpu.VMEM((tokens, pair), bf),
                pltpu.VMEM((tokens, pair), bf),
                pltpu.VMEM((keys, HEAD), f32),
                pltpu.VMEM((keys, HEAD), f32),
            ]
            + [pltpu.VMEM((slab, GROUP * BLOCK), t) for t in (f32, f32, bf, bf, bf, bf)],
        ),
        out_shape=out_shape,
        compiler_params=pltpu.CompilerParams(vmem_limit_bytes=VMEM_LIMIT),
        cost_estimate=HEAVY if chunk else LIGHT,
        name="attention",
    )(place, opened, lo, *own, near, near, near, halo[0], halo[0], halo[1], halo[1], grad_out, near, *far_do)


def sum_kernel(heads, sc_ref, near, far, *refs):
    dk, dv = refs[-2:]
    for g in range(heads):
        at = 2 * g * HEAD
        to = slice(g * HEAD, g * HEAD + HEAD)
        for out, col in ((dk, at), (dv, at + HEAD)):
            terms = [x[:, col : col + HEAD].astype(jnp.float32) for x in (near, far)]
            out[:, to] = (terms[0] + terms[1]).astype(out.dtype)


def sum_terms(place, chunk, side, heads, n_heads, terms, before, after=()):
    rows = terms[0].shape[0]
    wide = 2 * heads * HEAD
    by_core = terms[1].shape[0] > rows

    def at_near(n, sc):
        return (0, side)

    def at_far(n, sc):
        return (sc[0] if by_core else 0, 0)

    def at_out(n, sc):
        return (0, 2 * chunk + (sc[0] if side == 0 else 1 - sc[0]))

    shape = jax.ShapeDtypeStruct((rows, n_heads * HEAD), jnp.bfloat16)
    hbm = pl.BlockSpec(memory_space=pl.ANY)
    return pl.pallas_call(
        functools.partial(sum_kernel, heads),
        grid_spec=pltpu.PrefetchScalarGridSpec(
            num_scalar_prefetch=1,
            grid=(1,),
            in_specs=[pl.BlockSpec((rows, wide), at) for at in (at_near, at_far)]
            + [hbm] * len((*before, *after)),
            out_specs=[pl.BlockSpec((rows, heads * HEAD), at_out)] * 2,
        ),
        out_shape=[shape, shape],
        input_output_aliases={3: 0, 4: 1} if before else {},
        compiler_params=pltpu.CompilerParams(vmem_limit_bytes=VMEM_LIMIT),
        cost_estimate=LIGHT,
        name="sum_terms",
    )(place, *terms, *before, *after)


def body(queries, keys, values, grad_out, band_mask, segment_ids):
    n_ctx, n_mp = lax.axis_size("ctx"), lax.axis_size("mp")
    rows = queries.shape[0]
    piece = rows // n_mp
    heads_mp = KV_HEADS // n_mp
    heads = heads_mp // (2 * CHUNKS)
    pair = GROUP * HEAD
    wide = heads * pair
    bf = jnp.bfloat16
    ctx, mp = lax.axis_index("ctx"), lax.axis_index("mp")
    core, chip = lax.rem(ctx, 2), ctx // 2
    place = jnp.stack([core, mp]).astype(jnp.int32)

    def send(x, target):
        return lax.ppermute(x, AXES, routes(target, n_ctx, n_mp))

    swap = lambda c, m: (c ^ 1, m)

    def first_head(chunk, core):
        return (2 * chunk + core) * heads

    def col(head, width):
        return pl.multiple_of(head * width, HEAD)

    def plan_halo(chunk):
        def plan(core, mp):
            jobs, by = [], heads * HEAD
            for side in range(2):
                src = col(first_head(chunk, core if side == 0 else 1 - core), HEAD)
                for n in range(2):
                    dst, to = (side, n) if chunk == 0 else (0, 2 * side + n)
                    jobs.append((n, dst, (0, src), (0, to * by), (rows, by)))
            return jobs

        return plan

    def pack_halo(chunk, after):
        shapes = [(rows, wide)] * 2 if chunk == 0 else [(rows, 2 * wide)]
        return gather(plan_halo(chunk), 4, place, (keys, values), shapes, HEAVY, after, "pack_halo")

    far = [(dk, dm) for dm in range(1, n_mp) for dk in range(2)]
    n_far = n_mp - 1

    def plan_near(core, mp):
        jobs = []
        for dm in range(1, n_mp):
            mp_to = lax.rem(mp + dm, n_mp)
            for i in range(CHUNKS):
                for side in range(2):
                    core_to = core if side == 0 else 1 - core
                    src = col(mp_to * heads_mp + first_head(i, core_to), pair)
                    at = i * n_far + dm - 1
                    jobs.append((3, at, (0, src), (0, side * wide), (piece, wide)))
        for n, width, to in ((0, pair, 0), (1, HEAD, CHUNKS * wide), (2, HEAD, 3 * CHUNKS * wide // 2)):
            for i in range(CHUNKS):
                src = col(first_head(i, 1 - core), width)
                by = heads * width
                jobs.append((n, CHUNKS * n_far, (0, src), (0, to + i * by), (rows, by)))
        for i in range(CHUNKS):
            src = col(mp * heads_mp + first_head(i, 1 - core), pair)
            jobs.append((3, CHUNKS * n_far, (0, src), (i * piece, 2 * CHUNKS * wide), (piece, wide)))
        return jobs

    halos = [pack_halo(0, ())]
    *far_do, near = gather(
        plan_near,
        CHUNKS * (2 * n_far + 4),
        place,
        (queries, keys, values, grad_out),
        [(piece, 2 * wide)] * (CHUNKS * n_far) + [(rows, (2 * CHUNKS + 1) * wide)],
        HEAVY,
        halos[0],
        "pack_near",
    )
    far_do = [
        [
            send(far_do[i * n_far + dm - 1], lambda c, m: (c, (m + dm) % n_mp))
            for dm in range(1, n_mp)
        ]
        for i in range(CHUNKS)
    ]
    halos += [pack_halo(i, (near,)) for i in range(1, CHUNKS)]
    halo_in = [
        [send(x, lambda c, m: ((c + 2) ^ side, m)) for side, x in enumerate(halo)] for halo in halos
    ]
    near = send(near, swap)

    tokens = 2 * rows
    padded = jnp.concatenate([jnp.full((WINDOW,), -1, jnp.int32), segment_ids])
    ids = lax.dynamic_slice_in_dim(padded, chip * tokens, WINDOW + tokens, 0)
    before = jnp.sum((ids[:, None] < ids[None, WINDOW:]).astype(jnp.int32), axis=0)
    lo = jnp.maximum(before, jnp.arange(1, tokens + 1, dtype=jnp.int32))[None, :]
    blocks = tokens // BLOCK
    opened = lax.dynamic_slice_in_dim(band_mask, chip * blocks, blocks, 0).reshape(-1)

    out_parts, dq_parts, across_parts, near_parts, far_parts = [], [], [], [], []
    for i in range(CHUNKS):
        halo, ahead = halo_in[i], halos[i + 1 :]
        if i:
            halo, far_do[i], dq_parts = lax.optimization_barrier((halo, far_do[i], dq_parts))
        else:
            far_do[i], ahead, lo, opened = lax.optimization_barrier((far_do[i], ahead, lo, opened))
        halo = (halo[0], halo[1] if i == 0 else send(halo[0], swap))
        last = i == CHUNKS - 1
        dq_same, dkv_same, across, o_own, *o_far = attention(
            n_mp,
            rows,
            not last,
            i,
            heads,
            place,
            opened,
            lo,
            (queries, keys, values),
            near,
            halo,
            grad_out,
            [y for x in far_do[i] for y in (x, send(x, swap))],
        )
        n_far_o = 2 * n_mp - 2
        o_far, back = o_far[:n_far_o], o_far[n_far_o:]
        if i:
            earlier = (out_parts[-1], far_parts[-1])
            (back, o_far, across), earlier = lax.optimization_barrier(((back, o_far, across), earlier))
            out_parts[-1], far_parts[-1] = earlier
        if last:
            far_parts.append(
                [
                    send(back[0], lambda c, m: (c - 2, m)),
                    send(back[1], lambda c, m: ((c - 2) ^ 1 if c >= 2 else -1, m)),
                ]
            )
        else:
            far_parts.append([send(back[0], lambda c, m: (c - 2, m))])
        o_parts = [o_own]
        for dm in range(1, n_mp):
            o_parts.append(send(o_far[2 * dm - 2], lambda c, m: (c, (m + dm) % n_mp)))
            o_parts.append(send(o_far[2 * dm - 1], lambda c, m: (c ^ 1, (m + dm) % n_mp)))
        out_parts.append(o_parts)
        across_parts.append(send(across, swap))
        dq_parts.append(dq_same)
        near_parts.append(dkv_same)

    arrays = [
        x for o, a, q in zip(out_parts, across_parts, dq_parts) for x in (*o, a, q)
    ]

    def plan_out(core, mp):
        jobs, at = [], 0
        for i in range(CHUNKS):
            for dk, dm in [(0, 0)] + far:
                mp_from, core_from = lax.rem(mp + n_mp - dm, n_mp), core if dk == 0 else 1 - core
                to = col(mp_from * heads_mp + first_head(i, core_from), pair)
                jobs.append((at, 0, (0, 0), (0, to), (piece, wide)))
                at += 1
            to = col(mp * heads_mp + first_head(i, 1 - core), pair)
            rows_at = pl.multiple_of(mp * piece, piece)
            jobs.append((at, 0, (rows_at, 2 * wide), (0, to), (piece, wide)))
            to = col(first_head(i, 1 - core), pair)
            jobs.append((at, 1, (0, 0), (0, to), (rows, wide)))
            to = col(first_head(i, core), pair)
            jobs.append((at + 1, 1, (0, 0), (0, to), (rows, wide)))
            at += 2
        return jobs

    attn_out, grad_queries = gather(
        plan_out,
        CHUNKS * (len(far) + 4),
        place,
        arrays,
        [(piece, n_mp * heads_mp * pair), (rows, heads_mp * pair)],
        LIGHT,
        (),
        "put_together",
    )

    grads_kv = ()
    for i in range(CHUNKS):
        far_i = far_parts[i] if len(far_parts[i]) > 1 else [*far_parts[i], send(far_parts[i][0], swap)]
        for side, near_i in enumerate((near_parts[i], across_parts[i])):
            after = (attn_out,) if i == CHUNKS - 1 and side == 1 else ()
            terms = (near_i, far_i[side])
            grads_kv = sum_terms(place, i, side, heads, heads_mp, terms, grads_kv, after)
    return attn_out, grad_queries, grads_kv[0], grads_kv[1]


def solution(mesh):
    placed = (P("ctx", "mp"), P("ctx", "mp"), P("ctx", "mp"), P(("ctx", "mp"), None), P(), P())
    return jax.shard_map(
        body,
        mesh=mesh,
        in_specs=placed,
        out_specs=(P(("ctx", "mp"), None), P("ctx", "mp"), P("ctx", "mp"), P("ctx", "mp")),
        check_vma=False,
    )
```

```python
import functools
import math

import jax
import jax.numpy as jnp
from jax import lax
from jax.experimental import pallas as pl
from jax.experimental.pallas import tpu as pltpu
from jax.sharding import PartitionSpec as P

KV_HEADS = 16
GROUP = 2
HEAD = 128
WINDOW = 1024
BLOCK = 128
SPAN = WINDOW // BLOCK + 1
CHUNKS = 2
ATTN_SCALE = 168.0 ** (-0.5)
EXP2_SCALE = ATTN_SCALE * math.log2(math.e)
MASKED = -1e30
FAR = 1 << 20
AXES = ("ctx", "mp")
NT = (((1,), (1,)), ((), ()))
NN = (((1,), (0,)), ((), ()))
LIGHT = pl.CostEstimate(flops=0, bytes_accessed=1024, transcendentals=0)
VMEM_LIMIT = (64 * 1024 - 128) * 1024
HEAVY = pl.CostEstimate(flops=25_000_000_000, bytes_accessed=1024, transcendentals=0)


def dot(a, b, dims=NN):
    return lax.dot_general(a, b, dims, preferred_element_type=jnp.float32)


def routes(target, n_ctx, n_mp):
    out = []
    for c in range(n_ctx):
        for m in range(n_mp):
            d = target(c, m)
            if 0 <= d[0] < n_ctx:
                out.append((c * n_mp + m, d[0] * n_mp + d[1]))
    return out


def gather_kernel(plan, n_in, shapes, *refs):
    n = len(shapes)
    outs, images, sems = refs[n_in : n_in + n], refs[n_in + n : n_in + 2 * n], refs[-2:]
    into = [[] for _ in shapes]
    count = 0
    for src, dst, src_at, dst_at, size in plan(lax.rem(lax.axis_index("ctx"), 2), lax.axis_index("mp")):
        copy = pltpu.make_async_copy(
            refs[src].at[tuple(pl.ds(at, by) for at, by in zip(src_at, size))],
            images[dst].at[tuple(pl.ds(at, by) for at, by in zip(dst_at, size))],
            sems[0].at[count],
        )
        copy.start()
        into[dst].append(copy)
        count += 1
    written = []
    for dst in range(n):
        for copy in into[dst]:
            copy.wait()
        written.append(pltpu.make_async_copy(images[dst], outs[dst], sems[1].at[dst]))
        written[-1].start()
    for copy in written:
        copy.wait()


def gather(plan, count, arrays, shapes, cost, after=(), name="gather"):
    hbm = pl.BlockSpec(memory_space=pl.ANY)
    return pl.pallas_call(
        functools.partial(gather_kernel, plan, len(arrays) + len(after), shapes),
        in_specs=[hbm] * (len(arrays) + len(after)),
        out_specs=[hbm] * len(shapes),
        out_shape=[jax.ShapeDtypeStruct(shape, jnp.bfloat16) for shape in shapes],
        scratch_shapes=[pltpu.VMEM(shape, jnp.bfloat16) for shape in shapes]
        + [pltpu.SemaphoreType.DMA((count,)), pltpu.SemaphoreType.DMA((len(shapes),))],
        compiler_params=pltpu.CompilerParams(vmem_limit_bytes=VMEM_LIMIT),
        cost_estimate=cost,
        name=name,
    )(*arrays, *after)


def attention_kernel(n_mp, rows, whole, sc_ref, open_ref, lo_ref, *refs):
    q_own, k_own, v_own, q_near, k_near, v_near = refs[:6]
    kh_same, vh_same, kh_oth, vh_oth, do_own, do_oth = refs[6:12]
    do_far = refs[12 : 10 + 2 * n_mp]
    refs = refs[10 + 2 * n_mp :]
    n_back = 1 if whole else 2
    dq_same, dkv_same, across, o_own, o_oth, *o_far = refs[: 3 + 2 * n_mp]
    back = refs[3 + 2 * n_mp : 3 + 2 * n_mp + n_back]
    refs = refs[3 + 2 * n_mp + n_back :]
    qs, ks, vs, k_t, v_t, dos, os, dqs, dk, dv = refs[:10]
    s_refs, e_refs, ds_refs = refs[-6:-4], refs[-4:-2], refs[-2:]
    core, mp = sc_ref[0], sc_ref[1]
    piece, pair = rows // n_mp, GROUP * HEAD
    same = pl.ds(pl.multiple_of(core * rows, rows), rows)
    oth = pl.ds(pl.multiple_of((1 - core) * rows, rows), rows)
    same_kv = pl.ds(pl.multiple_of(WINDOW + core * rows, rows), rows)
    oth_kv = pl.ds(pl.multiple_of(WINDOW + (1 - core) * rows, rows), rows)

    def piece_at(dk_, dm):
        k_at = core if dk_ == 0 else 1 - core
        return pl.ds(pl.multiple_of(k_at * rows + lax.rem(mp + dm, n_mp) * piece, piece), piece)

    qs[same, :] = q_own[...]
    qs[oth, :] = q_near[...]
    ks[same, :] = kh_same[...]
    ks[oth, :] = kh_oth[...]
    ks[same_kv, :] = k_own[...]
    ks[oth_kv, :] = k_near[...]
    vs[same, :] = vh_same[...]
    vs[oth, :] = vh_oth[...]
    vs[same_kv, :] = v_own[...]
    vs[oth_kv, :] = v_near[...]
    dos[piece_at(0, 0), :] = do_own[...]
    dos[piece_at(1, 0), :] = do_oth[...]
    for at in range(n_mp - 1):
        dos[piece_at(0, n_mp - 1 - at), :] = do_far[2 * at][...]
        dos[piece_at(1, n_mp - 1 - at), :] = do_far[2 * at + 1][...]
    dk[...] = jnp.zeros_like(dk)
    dv[...] = jnp.zeros_like(dv)
    for t in range(ks.shape[0] // 256):
        at = slice(t * 256, t * 256 + 256)
        k_t[:, at] = ks[at, :].T
        v_t[:, at] = vs[at, :].T

    width = GROUP * BLOCK
    row = lax.broadcasted_iota(jnp.int32, (BLOCK, width), 0)
    lane = lax.broadcasted_iota(jnp.int32, (BLOCK, width), 1)
    causal = row <= lax.rem(lane, BLOCK)

    def by_rows(x, reduce):
        return reduce(x.reshape(BLOCK // 8, 8, width), axis=0)

    def forward(b):
        s_ref, e_ref = s_refs[b % 2], e_refs[b % 2]
        at_q = slice(b * BLOCK, b * BLOCK + BLOCK)
        q_blk = jnp.concatenate([qs[at_q, :HEAD], qs[at_q, HEAD:]], axis=0)
        lo = jnp.concatenate([lo_ref[:, at_q]] * GROUP, axis=1)
        top = jnp.full((8, width), MASKED, jnp.float32)
        for j in range(SPAN):
            part = slice(j * BLOCK, j * BLOCK + BLOCK)
            s = dot(ks[(b + j) * BLOCK : (b + j + 1) * BLOCK, :], q_blk, NT)
            closed = jnp.where(open_ref[b * SPAN + SPAN - 1 - j] == 1, 0, FAR)
            valid = row >= jnp.maximum(lo - (b + j) * BLOCK, closed)
            if j == SPAN - 1:
                valid = valid & causal
            s = jnp.where(valid, s, MASKED)
            s_ref[part, :] = s
            top = jnp.maximum(top, by_rows(s, jnp.max))
        top = jnp.max(top, axis=0, keepdims=True)
        total = jnp.zeros((8, width), jnp.float32)
        for j in range(SPAN):
            part = slice(j * BLOCK, j * BLOCK + BLOCK)
            e = jnp.exp2((s_ref[part, :] - top) * EXP2_SCALE)
            total = total + by_rows(e, jnp.sum)
            e_ref[part, :] = e.astype(jnp.bfloat16)
        return q_blk, 1.0 / jnp.sum(total, axis=0, keepdims=True)

    def backward(b, q_blk, inverse):
        e_ref, ds_ref = e_refs[b % 2], ds_refs[b % 2]
        at_q = slice(b * BLOCK, b * BLOCK + BLOCK)
        at_keys = slice(b * BLOCK, (b + SPAN) * BLOCK)
        o_t = (dot(v_t[:, at_keys], e_ref[...]) * inverse).astype(jnp.bfloat16)
        os[at_q, :HEAD] = o_t[:, :BLOCK].T
        os[at_q, HEAD:] = o_t[:, BLOCK:].T
        do_t = jnp.concatenate([dos[at_q, :HEAD].T, dos[at_q, HEAD:].T], axis=1)
        do_t = (do_t.astype(jnp.float32) * inverse).astype(jnp.bfloat16)
        delta = jnp.sum(
            do_t.astype(jnp.float32) * o_t.astype(jnp.float32), axis=0, keepdims=True
        )
        for j in range(SPAN):
            part = slice(j * BLOCK, j * BLOCK + BLOCK)
            dp = dot(vs[(b + j) * BLOCK : (b + j + 1) * BLOCK, :], do_t)
            ds_ref[part, :] = (e_ref[part, :].astype(jnp.float32) * (dp - delta)).astype(
                jnp.bfloat16
            )
        dv[at_keys, :] += dot(e_ref[...], do_t, NT)
        dk[at_keys, :] += dot(ds_ref[...], q_blk)
        dq_t = (dot(k_t[:, at_keys], ds_ref[...]) * ATTN_SCALE).astype(jnp.bfloat16)
        dqs[at_q, :HEAD] = dq_t[:, :BLOCK].T
        dqs[at_q, HEAD:] = dq_t[:, BLOCK:].T

    blocks = qs.shape[0] // BLOCK
    ahead = forward(0)
    for b in range(blocks):
        now, ahead = ahead, forward(b + 1) if b + 1 < blocks else None
        backward(b, *now)

    dq_same[...] = dqs[same, :]
    wide = across.shape[1] // 2
    at_g = pl.multiple_of(pl.program_id(0) * pair, pair)
    across[:, pl.ds(at_g, pair)] = dqs[oth, :]
    o_own[...] = os[piece_at(0, 0), :]
    o_oth[...] = os[piece_at(1, 0), :]
    for at in range(n_mp - 1):
        o_far[2 * at][...] = os[piece_at(0, at + 1), :]
        o_far[2 * at + 1][...] = os[piece_at(1, at + 1), :]
    ats = (slice(0, 2 * rows),) if whole else (same, oth)
    for out, at in ((dkv_same, same_kv), *zip(back, ats)):
        out[:, :HEAD] = (dk[at, :] * ATTN_SCALE).astype(out.dtype)
        out[:, HEAD:] = dv[at, :].astype(out.dtype)
    across[:, pl.ds(wide + at_g, HEAD)] = (dk[oth_kv, :] * ATTN_SCALE).astype(across.dtype)
    across[:, pl.ds(wide + at_g + HEAD, HEAD)] = dv[oth_kv, :].astype(across.dtype)


def attention(n_mp, rows, whole, chunk, heads, place, opened, lo, own, near, halo, grad_out, far_do):
    heads_mp = 2 * CHUNKS * heads
    piece, pair = rows // n_mp, GROUP * HEAD
    heads_chunk, first = heads, chunk * heads

    def at_head(g, sc, *unused):
        return (0, 2 * first + sc[0] * heads + g)

    def at_grad(g, sc, *unused):
        return (0, sc[1] * heads_mp + 2 * first + sc[0] * heads + g)

    def at_near(column):
        return lambda g, *unused: (0, column + first + g)

    def at_near_do(g, *unused):
        return (chunk, CHUNKS * 2 * heads + g)

    def at_halo(which, side):
        skip = 2 * heads if side and chunk else 0
        return lambda g, *unused: (0, skip + which * heads + g)

    def at_local(g, *unused):
        return (0, g)

    def at_handed(g, *unused):
        return (0, heads + g)

    in_specs = [pl.BlockSpec((1, 2 * rows), lambda g, *unused: (0, 0))]
    in_specs += [pl.BlockSpec((rows, pair), at_head)]
    in_specs += [pl.BlockSpec((rows, HEAD), at_head)] * 2
    in_specs += [pl.BlockSpec((rows, pair), at_near(0))]
    in_specs += [pl.BlockSpec((rows, HEAD), at_near(n * CHUNKS * heads)) for n in (2, 3)]
    in_specs += [pl.BlockSpec((rows, HEAD), at_halo(n % 2, n // 2)) for n in range(4)]
    in_specs += [pl.BlockSpec((piece, pair), at_grad), pl.BlockSpec((piece, pair), at_near_do)]
    in_specs += [pl.BlockSpec((piece, pair), at) for at in (at_local, at_handed)] * (n_mp - 1)
    wide = heads_chunk * pair
    bf, f32 = jnp.bfloat16, jnp.float32
    out_specs = [pl.BlockSpec((rows, pair), at_local)] * 2
    out_specs += [pl.BlockSpec((rows, 2 * wide), lambda g, *unused: (0, 0))]
    out_specs += [pl.BlockSpec((piece, pair), at_local)] * (2 * n_mp)
    out_shape = [jax.ShapeDtypeStruct((rows, wide), bf)] * 2
    out_shape += [jax.ShapeDtypeStruct((rows, 2 * wide), bf)]
    out_shape += [jax.ShapeDtypeStruct((piece, wide), bf)] * (2 * n_mp)
    n_back, rows_back = (1, 2 * rows) if whole else (2, rows)
    out_specs += [pl.BlockSpec((rows_back, pair), at_local)] * n_back
    out_shape += [jax.ShapeDtypeStruct((rows_back, wide), bf)] * n_back
    tokens, keys, slab = 2 * rows, WINDOW + 2 * rows, SPAN * BLOCK
    return pl.pallas_call(
        functools.partial(attention_kernel, n_mp, rows, whole),
        grid_spec=pltpu.PrefetchScalarGridSpec(
            num_scalar_prefetch=2,
            grid=(heads_chunk,),
            in_specs=in_specs,
            out_specs=out_specs,
            scratch_shapes=[
                pltpu.VMEM((tokens, pair), bf),
                pltpu.VMEM((keys, HEAD), bf),
                pltpu.VMEM((keys, HEAD), bf),
                pltpu.VMEM((HEAD, keys), bf),
                pltpu.VMEM((HEAD, keys), bf),
                pltpu.VMEM((tokens, pair), bf),
                pltpu.VMEM((tokens, pair), bf),
                pltpu.VMEM((tokens, pair), bf),
                pltpu.VMEM((keys, HEAD), f32),
                pltpu.VMEM((keys, HEAD), f32),
            ]
            + [pltpu.VMEM((slab, GROUP * BLOCK), t) for t in (f32, f32, bf, bf, bf, bf)],
        ),
        out_shape=out_shape,
        compiler_params=pltpu.CompilerParams(vmem_limit_bytes=VMEM_LIMIT),
        cost_estimate=HEAVY if chunk else LIGHT,
        name="attention",
    )(place, opened, lo, *own, near, near, near, halo[0], halo[0], halo[1], halo[1], grad_out, near, *far_do)


def sum_kernel(heads, sc_ref, *refs):
    dk, dv = refs[-2:]
    core = sc_ref[0]
    for at in range(heads * 2):
        near, far = refs[2 * at : 2 * at + 2]
        half = core if at % 2 == 0 else 1 - core
        to = pl.ds(pl.multiple_of((half * heads + at // 2) * HEAD, HEAD), HEAD)
        total = near[...].astype(jnp.float32) + far[...].astype(jnp.float32)
        dk[:, to] = total[:, :HEAD].astype(dk.dtype)
        dv[:, to] = total[:, HEAD:].astype(dv.dtype)


def sum_terms(place, chunk, heads, n_heads, terms, before, after):
    pair = 2 * HEAD
    rows = terms[0][0].shape[0]
    hbm = pl.BlockSpec(memory_space=pl.ANY)

    def spec(x, by_core, column):
        return pl.BlockSpec((rows, pair), lambda g, sc: (sc[0] if by_core else 0, column))

    shape = jax.ShapeDtypeStruct((rows, n_heads * HEAD), jnp.bfloat16)
    return pl.pallas_call(
        functools.partial(sum_kernel, heads),
        grid_spec=pltpu.PrefetchScalarGridSpec(
            num_scalar_prefetch=1,
            grid=(1,),
            in_specs=[spec(*t) for t in terms] + [hbm] * len((*before, *after)),
            out_specs=[pl.BlockSpec((rows, 2 * heads * HEAD), lambda g, sc: (0, chunk))] * 2,
        ),
        out_shape=[shape, shape],
        input_output_aliases={len(terms) + 1: 0, len(terms) + 2: 1} if before else {},
        compiler_params=pltpu.CompilerParams(vmem_limit_bytes=VMEM_LIMIT),
        cost_estimate=LIGHT,
        name="sum_terms",
    )(place, *[t[0] for t in terms], *before, *after)


def body(queries, keys, values, grad_out, band_mask, segment_ids):
    n_ctx, n_mp = lax.axis_size("ctx"), lax.axis_size("mp")
    rows = queries.shape[0]
    piece = rows // n_mp
    heads_mp = KV_HEADS // n_mp
    heads = heads_mp // (2 * CHUNKS)
    pair = GROUP * HEAD
    wide = heads * pair
    bf = jnp.bfloat16
    ctx, mp = lax.axis_index("ctx"), lax.axis_index("mp")
    core, chip = lax.rem(ctx, 2), ctx // 2
    place = jnp.stack([core, mp]).astype(jnp.int32)

    def send(x, target):
        return lax.ppermute(x, AXES, routes(target, n_ctx, n_mp))

    swap = lambda c, m: (c ^ 1, m)

    def first_head(chunk, core):
        return (2 * chunk + core) * heads

    def col(head, width):
        return pl.multiple_of(head * width, HEAD)

    def plan_halo(chunk):
        def plan(core, mp):
            jobs, by = [], heads * HEAD
            for side in range(2):
                src = col(first_head(chunk, core if side == 0 else 1 - core), HEAD)
                for n in range(2):
                    dst, to = (side, n) if chunk == 0 else (0, 2 * side + n)
                    jobs.append((n, dst, (0, src), (0, to * by), (rows, by)))
            return jobs

        return plan

    def pack_halo(chunk, after):
        shapes = [(rows, wide)] * 2 if chunk == 0 else [(rows, 2 * wide)]
        return gather(plan_halo(chunk), 4, (keys, values), shapes, HEAVY, after, "pack_halo")

    far = [(dk, dm) for dm in range(1, n_mp) for dk in range(2)]
    n_far = n_mp - 1

    def plan_near(core, mp):
        jobs = []
        for dm in range(1, n_mp):
            mp_to = lax.rem(mp + dm, n_mp)
            for i in range(CHUNKS):
                for side in range(2):
                    core_to = core if side == 0 else 1 - core
                    src = col(mp_to * heads_mp + first_head(i, core_to), pair)
                    at = i * n_far + dm - 1
                    jobs.append((3, at, (0, src), (0, side * wide), (piece, wide)))
        for n, width, to in ((0, pair, 0), (1, HEAD, CHUNKS * wide), (2, HEAD, 3 * CHUNKS * wide // 2)):
            for i in range(CHUNKS):
                src = col(first_head(i, 1 - core), width)
                by = heads * width
                jobs.append((n, CHUNKS * n_far, (0, src), (0, to + i * by), (rows, by)))
        for i in range(CHUNKS):
            src = col(mp * heads_mp + first_head(i, 1 - core), pair)
            jobs.append((3, CHUNKS * n_far, (0, src), (i * piece, 2 * CHUNKS * wide), (piece, wide)))
        return jobs

    halos = [pack_halo(0, ())]
    *far_do, near = gather(
        plan_near,
        CHUNKS * (2 * n_far + 4),
        (queries, keys, values, grad_out),
        [(piece, 2 * wide)] * (CHUNKS * n_far) + [(rows, (2 * CHUNKS + 1) * wide)],
        HEAVY,
        halos[0],
        "pack_near",
    )
    far_do = [
        [
            send(far_do[i * n_far + dm - 1], lambda c, m: (c, (m + dm) % n_mp))
            for dm in range(1, n_mp)
        ]
        for i in range(CHUNKS)
    ]
    halos += [pack_halo(i, (near,)) for i in range(1, CHUNKS)]
    halo_in = [
        [send(x, lambda c, m: ((c + 2) ^ side, m)) for side, x in enumerate(halo)] for halo in halos
    ]
    near = send(near, swap)

    tokens = 2 * rows
    padded = jnp.concatenate([jnp.full((WINDOW,), -1, jnp.int32), segment_ids])
    ids = lax.dynamic_slice_in_dim(padded, chip * tokens, WINDOW + tokens, 0)
    before = jnp.sum((ids[:, None] < ids[None, WINDOW:]).astype(jnp.int32), axis=0)
    lo = jnp.maximum(before, jnp.arange(1, tokens + 1, dtype=jnp.int32))[None, :]
    blocks = tokens // BLOCK
    opened = lax.dynamic_slice_in_dim(band_mask, chip * blocks, blocks, 0).reshape(-1)

    out_parts, dq_parts, across_parts, near_parts, far_parts = [], [], [], [], []
    for i in range(CHUNKS):
        halo, ahead = halo_in[i], halos[i + 1 :]
        if i:
            halo, far_do[i], dq_parts = lax.optimization_barrier((halo, far_do[i], dq_parts))
        else:
            far_do[i], ahead, lo, opened = lax.optimization_barrier((far_do[i], ahead, lo, opened))
        halo = (halo[0], halo[1] if i == 0 else send(halo[0], swap))
        last = i == CHUNKS - 1
        dq_same, dkv_same, across, o_own, *o_far = attention(
            n_mp,
            rows,
            not last,
            i,
            heads,
            place,
            opened,
            lo,
            (queries, keys, values),
            near,
            halo,
            grad_out,
            [y for x in far_do[i] for y in (x, send(x, swap))],
        )
        n_far_o = 2 * n_mp - 1
        o_far, back = o_far[:n_far_o], o_far[n_far_o:]
        if i:
            earlier = (out_parts[-1], across_parts[-1])
            (back, o_far, across), earlier = lax.optimization_barrier(((back, o_far, across), earlier))
            out_parts[-1], across_parts[-1] = earlier
        if last:
            far_parts.append(
                [
                    send(back[0], lambda c, m: (c - 2, m)),
                    send(back[1], lambda c, m: ((c - 2) ^ 1 if c >= 2 else -1, m)),
                ]
            )
        else:
            far_parts.append([send(back[0], lambda c, m: (c - 2, m))])
        o_parts = [
            send(o_far[1 + at], lambda c, m: (c ^ dk, (m + dm) % n_mp))
            for at, (dk, dm) in enumerate(far)
        ]
        o_oth = o_far[0]
        if last:
            o_oth, o_parts[0] = lax.optimization_barrier((o_oth, o_parts[0]))
        out_parts.append([o_own, send(o_oth, swap), *o_parts])
        across_parts.append(send(across, swap))
        dq_parts.append(dq_same)
        near_parts.append(dkv_same)

    arrays = [
        x for o, a, q in zip(out_parts, across_parts, dq_parts) for x in (*o, a, q)
    ]

    def plan_out(core, mp):
        jobs, at = [], 0
        for i in range(CHUNKS):
            for dk, dm in [(0, 0), (1, 0)] + far:
                mp_from, core_from = lax.rem(mp + n_mp - dm, n_mp), core if dk == 0 else 1 - core
                to = col(mp_from * heads_mp + first_head(i, core_from), pair)
                jobs.append((at, 0, (0, 0), (0, to), (piece, wide)))
                at += 1
            to = col(first_head(i, 1 - core), pair)
            jobs.append((at, 1, (0, 0), (0, to), (rows, wide)))
            to = col(first_head(i, core), pair)
            jobs.append((at + 1, 1, (0, 0), (0, to), (rows, wide)))
            at += 2
        return jobs

    attn_out, grad_queries = gather(
        plan_out,
        CHUNKS * (len(far) + 4),
        arrays,
        [(piece, n_mp * heads_mp * pair), (rows, heads_mp * pair)],
        LIGHT,
        (),
        "put_together",
    )

    grads_kv = ()
    for i in range(CHUNKS):
        terms = []
        if i < CHUNKS - 1:
            back, far_parts[-1][0] = lax.optimization_barrier((far_parts[i][0], far_parts[-1][0]))
            handed = [
                send(lax.dynamic_slice(back, ((1 - core) * rows, g * pair), (rows, pair)), swap)
                for g in range(heads)
            ]
        for g in range(heads):
            last = i == CHUNKS - 1
            terms += [(near_parts[i], False, g), (far_parts[i][0], not last, g)]
            terms += [(across_parts[i], False, heads + g)]
            terms += [(far_parts[i][1], False, g) if last else (handed[g], False, 0)]
        grads_kv = sum_terms(place, i, heads, heads_mp, terms, grads_kv, (attn_out,))
    return attn_out, grad_queries, grads_kv[0], grads_kv[1]


def solution(mesh):
    placed = (P("ctx", "mp"), P("ctx", "mp"), P("ctx", "mp"), P(("ctx", "mp"), None), P(), P())
    return jax.shard_map(
        body,
        mesh=mesh,
        in_specs=placed,
        out_specs=(P(("ctx", "mp"), None), P("ctx", "mp"), P("ctx", "mp"), P("ctx", "mp")),
        check_vma=False,
    )
```

```python
import functools
import math

import jax
import jax.numpy as jnp
from jax import lax
from jax.experimental import pallas as pl
from jax.experimental.pallas import tpu as pltpu
from jax.sharding import PartitionSpec as P

KV_HEADS = 16
GROUP = 2
HEAD = 128
WINDOW = 1024
BLOCK = 128
SPAN = WINDOW // BLOCK + 1
CHUNKS = 2
ATTN_SCALE = 168.0 ** (-0.5)
EXP2_SCALE = ATTN_SCALE * math.log2(math.e)
MASKED = -1e30
FAR = 1 << 20
AXES = ("ctx", "mp")
NT = (((1,), (1,)), ((), ()))
NN = (((1,), (0,)), ((), ()))
LIGHT = pl.CostEstimate(flops=0, bytes_accessed=1024, transcendentals=0)
VMEM_LIMIT = (64 * 1024 - 128) * 1024
MEDIUM = pl.CostEstimate(flops=4_000_000_000, bytes_accessed=1024, transcendentals=0)
HEAVY = pl.CostEstimate(flops=25_000_000_000, bytes_accessed=1024, transcendentals=0)


def dot(a, b, dims=NN):
    return lax.dot_general(a, b, dims, preferred_element_type=jnp.float32)


def routes(target, n_ctx, n_mp):
    out = []
    for c in range(n_ctx):
        for m in range(n_mp):
            d = target(c, m)
            if 0 <= d[0] < n_ctx:
                out.append((c * n_mp + m, d[0] * n_mp + d[1]))
    return out


def gather_kernel(plan, n_in, shapes, *refs):
    n = len(shapes)
    outs, images, sems = refs[n_in : n_in + n], refs[n_in + n : n_in + 2 * n], refs[-2:]
    into = [[] for _ in shapes]
    count = 0
    for src, dst, src_at, dst_at, size in plan(lax.rem(lax.axis_index("ctx"), 2), lax.axis_index("mp")):
        copy = pltpu.make_async_copy(
            refs[src].at[tuple(pl.ds(at, by) for at, by in zip(src_at, size))],
            images[dst].at[tuple(pl.ds(at, by) for at, by in zip(dst_at, size))],
            sems[0].at[count],
        )
        copy.start()
        into[dst].append(copy)
        count += 1
    written = []
    for dst in range(n):
        for copy in into[dst]:
            copy.wait()
        written.append(pltpu.make_async_copy(images[dst], outs[dst], sems[1].at[dst]))
        written[-1].start()
    for copy in written:
        copy.wait()


def gather(plan, count, arrays, shapes, cost, after=(), name="gather"):
    hbm = pl.BlockSpec(memory_space=pl.ANY)
    return pl.pallas_call(
        functools.partial(gather_kernel, plan, len(arrays) + len(after), shapes),
        in_specs=[hbm] * (len(arrays) + len(after)),
        out_specs=[hbm] * len(shapes),
        out_shape=[jax.ShapeDtypeStruct(shape, jnp.bfloat16) for shape in shapes],
        scratch_shapes=[pltpu.VMEM(shape, jnp.bfloat16) for shape in shapes]
        + [pltpu.SemaphoreType.DMA((count,)), pltpu.SemaphoreType.DMA((len(shapes),))],
        compiler_params=pltpu.CompilerParams(vmem_limit_bytes=VMEM_LIMIT),
        cost_estimate=cost,
        name=name,
    )(*arrays, *after)


def attention_kernel(n_mp, rows, whole, sc_ref, open_ref, lo_ref, *refs):
    q_own, k_own, v_own, q_near, k_near, v_near = refs[:6]
    kh_same, vh_same, kh_oth, vh_oth, do_own, do_oth = refs[6:12]
    do_far = refs[12 : 10 + 2 * n_mp]
    refs = refs[10 + 2 * n_mp :]
    n_back = 1 if whole else 2
    dq_same, dkv_same, across, o_own, o_oth, *o_far = refs[: 3 + 2 * n_mp]
    back = refs[3 + 2 * n_mp : 3 + 2 * n_mp + n_back]
    refs = refs[3 + 2 * n_mp + n_back :]
    qs, ks, vs, k_t, v_t, dos, os, dqs, dk, dv = refs[:10]
    s_refs, e_refs, ds_refs = refs[-6:-4], refs[-4:-2], refs[-2:]
    core, mp = sc_ref[0], sc_ref[1]
    piece, pair = rows // n_mp, GROUP * HEAD
    same = pl.ds(pl.multiple_of(core * rows, rows), rows)
    oth = pl.ds(pl.multiple_of((1 - core) * rows, rows), rows)
    same_kv = pl.ds(pl.multiple_of(WINDOW + core * rows, rows), rows)
    oth_kv = pl.ds(pl.multiple_of(WINDOW + (1 - core) * rows, rows), rows)

    def piece_at(dk_, dm):
        k_at = core if dk_ == 0 else 1 - core
        return pl.ds(pl.multiple_of(k_at * rows + lax.rem(mp + dm, n_mp) * piece, piece), piece)

    qs[same, :] = q_own[...]
    qs[oth, :] = q_near[...]
    ks[same, :] = kh_same[...]
    ks[oth, :] = kh_oth[...]
    ks[same_kv, :] = k_own[...]
    ks[oth_kv, :] = k_near[...]
    vs[same, :] = vh_same[...]
    vs[oth, :] = vh_oth[...]
    vs[same_kv, :] = v_own[...]
    vs[oth_kv, :] = v_near[...]
    dos[piece_at(0, 0), :] = do_own[...]
    dos[piece_at(1, 0), :] = do_oth[...]
    for at in range(n_mp - 1):
        dos[piece_at(0, n_mp - 1 - at), :] = do_far[2 * at][...]
        dos[piece_at(1, n_mp - 1 - at), :] = do_far[2 * at + 1][...]
    for t in range(ks.shape[0] // 256):
        at = slice(t * 256, t * 256 + 256)
        k_t[:, at] = ks[at, :].T
        v_t[:, at] = vs[at, :].T

    width = GROUP * BLOCK
    row = lax.broadcasted_iota(jnp.int32, (BLOCK, width), 0)
    lane = lax.broadcasted_iota(jnp.int32, (BLOCK, width), 1)
    causal = row <= lax.rem(lane, BLOCK)

    def by_rows(x, reduce):
        return reduce(x.reshape(BLOCK // 8, 8, width), axis=0)

    def forward(b):
        s_ref, e_ref = s_refs[b % 2], e_refs[b % 2]
        at_q = slice(b * BLOCK, b * BLOCK + BLOCK)
        q_blk = jnp.concatenate([qs[at_q, :HEAD], qs[at_q, HEAD:]], axis=0)
        lo = jnp.concatenate([lo_ref[:, at_q]] * GROUP, axis=1)
        top = jnp.full((8, width), MASKED, jnp.float32)
        for j in range(SPAN):
            part = slice(j * BLOCK, j * BLOCK + BLOCK)
            s = dot(ks[(b + j) * BLOCK : (b + j + 1) * BLOCK, :], q_blk, NT)
            closed = jnp.where(open_ref[b * SPAN + SPAN - 1 - j] == 1, 0, FAR)
            valid = row >= jnp.maximum(lo - (b + j) * BLOCK, closed)
            if j == SPAN - 1:
                valid = valid & causal
            s = jnp.where(valid, s, MASKED)
            s_ref[part, :] = s
            top = jnp.maximum(top, by_rows(s, jnp.max))
        top = jnp.max(top, axis=0, keepdims=True)
        total = jnp.zeros((8, width), jnp.float32)
        for j in range(SPAN):
            part = slice(j * BLOCK, j * BLOCK + BLOCK)
            e = jnp.exp2((s_ref[part, :] - top) * EXP2_SCALE)
            total = total + by_rows(e, jnp.sum)
            e_ref[part, :] = e.astype(jnp.bfloat16)
        return q_blk, 1.0 / jnp.sum(total, axis=0, keepdims=True)

    def backward(b, q_blk, inverse):
        e_ref, ds_ref = e_refs[b % 2], ds_refs[b % 2]
        at_q = slice(b * BLOCK, b * BLOCK + BLOCK)
        at_keys = slice(b * BLOCK, (b + SPAN) * BLOCK)
        o_t = (dot(v_t[:, at_keys], e_ref[...]) * inverse).astype(jnp.bfloat16)
        os[at_q, :HEAD] = o_t[:, :BLOCK].T
        os[at_q, HEAD:] = o_t[:, BLOCK:].T
        do_t = jnp.concatenate([dos[at_q, :HEAD].T, dos[at_q, HEAD:].T], axis=1)
        do_t = (do_t.astype(jnp.float32) * inverse).astype(jnp.bfloat16)
        delta = jnp.sum(
            do_t.astype(jnp.float32) * o_t.astype(jnp.float32), axis=0, keepdims=True
        )
        for j in range(SPAN):
            part = slice(j * BLOCK, j * BLOCK + BLOCK)
            dp = dot(vs[(b + j) * BLOCK : (b + j + 1) * BLOCK, :], do_t)
            ds_ref[part, :] = (e_ref[part, :].astype(jnp.float32) * (dp - delta)).astype(
                jnp.bfloat16
            )
        for total, part in ((dv, dot(e_ref[...], do_t, NT)), (dk, dot(ds_ref[...], q_blk))):
            met = 0 if b == 0 else WINDOW
            seen, fresh = slice(b * BLOCK, b * BLOCK + met), slice(b * BLOCK + met, (b + SPAN) * BLOCK)
            if met:
                total[seen, :] += part[:met]
            total[fresh, :] = part[met:]
        dq_t = (dot(k_t[:, at_keys], ds_ref[...]) * ATTN_SCALE).astype(jnp.bfloat16)
        dqs[at_q, :HEAD] = dq_t[:, :BLOCK].T
        dqs[at_q, HEAD:] = dq_t[:, BLOCK:].T

    blocks = qs.shape[0] // BLOCK
    ahead = forward(0)
    for b in range(blocks):
        now, ahead = ahead, forward(b + 1) if b + 1 < blocks else None
        backward(b, *now)

    dq_same[...] = dqs[same, :]
    wide = across.shape[1] // 2
    at_g = pl.multiple_of(pl.program_id(0) * pair, pair)
    across[:, pl.ds(at_g, pair)] = dqs[oth, :]
    o_own[...] = os[piece_at(0, 0), :]
    o_oth[...] = os[piece_at(1, 0), :]
    for at in range(n_mp - 1):
        o_far[2 * at][...] = os[piece_at(0, at + 1), :]
        o_far[2 * at + 1][...] = os[piece_at(1, at + 1), :]
    ats = (slice(0, 2 * rows),) if whole else (same, oth)
    for out, at in ((dkv_same, same_kv), *zip(back, ats)):
        out[:, :HEAD] = (dk[at, :] * ATTN_SCALE).astype(out.dtype)
        out[:, HEAD:] = dv[at, :].astype(out.dtype)
    across[:, pl.ds(wide + at_g, HEAD)] = (dk[oth_kv, :] * ATTN_SCALE).astype(across.dtype)
    across[:, pl.ds(wide + at_g + HEAD, HEAD)] = dv[oth_kv, :].astype(across.dtype)


def attention(n_mp, rows, whole, chunk, heads, place, opened, lo, own, near, halo, grad_out, far_do):
    heads_mp = 2 * CHUNKS * heads
    piece, pair = rows // n_mp, GROUP * HEAD
    heads_chunk, first = heads, chunk * heads

    def at_head(g, sc, *unused):
        return (0, 2 * first + sc[0] * heads + g)

    def at_grad(g, sc, *unused):
        return (0, sc[1] * heads_mp + 2 * first + sc[0] * heads + g)

    def at_near(column):
        return lambda g, *unused: (0, column + first + g)

    def at_near_do(g, *unused):
        return (chunk, CHUNKS * 2 * heads + g)

    def at_halo(which, side):
        skip = 2 * heads if side and chunk else 0
        return lambda g, *unused: (0, skip + which * heads + g)

    def at_local(g, *unused):
        return (0, g)

    def at_handed(g, *unused):
        return (0, heads + g)

    in_specs = [pl.BlockSpec((1, 2 * rows), lambda g, *unused: (0, 0))]
    in_specs += [pl.BlockSpec((rows, pair), at_head)]
    in_specs += [pl.BlockSpec((rows, HEAD), at_head)] * 2
    in_specs += [pl.BlockSpec((rows, pair), at_near(0))]
    in_specs += [pl.BlockSpec((rows, HEAD), at_near(n * CHUNKS * heads)) for n in (2, 3)]
    in_specs += [pl.BlockSpec((rows, HEAD), at_halo(n % 2, n // 2)) for n in range(4)]
    in_specs += [pl.BlockSpec((piece, pair), at_grad), pl.BlockSpec((piece, pair), at_near_do)]
    in_specs += [pl.BlockSpec((piece, pair), at) for at in (at_local, at_handed)] * (n_mp - 1)
    wide = heads_chunk * pair
    bf, f32 = jnp.bfloat16, jnp.float32
    out_specs = [pl.BlockSpec((rows, pair), at_local)] * 2
    out_specs += [pl.BlockSpec((rows, 2 * wide), lambda g, *unused: (0, 0))]
    out_specs += [pl.BlockSpec((piece, pair), at_local)] * (2 * n_mp)
    out_shape = [jax.ShapeDtypeStruct((rows, wide), bf)] * 2
    out_shape += [jax.ShapeDtypeStruct((rows, 2 * wide), bf)]
    out_shape += [jax.ShapeDtypeStruct((piece, wide), bf)] * (2 * n_mp)
    n_back, rows_back = (1, 2 * rows) if whole else (2, rows)
    out_specs += [pl.BlockSpec((rows_back, pair), at_local)] * n_back
    out_shape += [jax.ShapeDtypeStruct((rows_back, wide), bf)] * n_back
    tokens, keys, slab = 2 * rows, WINDOW + 2 * rows, SPAN * BLOCK
    return pl.pallas_call(
        functools.partial(attention_kernel, n_mp, rows, whole),
        grid_spec=pltpu.PrefetchScalarGridSpec(
            num_scalar_prefetch=2,
            grid=(heads_chunk,),
            in_specs=in_specs,
            out_specs=out_specs,
            scratch_shapes=[
                pltpu.VMEM((tokens, pair), bf),
                pltpu.VMEM((keys, HEAD), bf),
                pltpu.VMEM((keys, HEAD), bf),
                pltpu.VMEM((HEAD, keys), bf),
                pltpu.VMEM((HEAD, keys), bf),
                pltpu.VMEM((tokens, pair), bf),
                pltpu.VMEM((tokens, pair), bf),
                pltpu.VMEM((tokens, pair), bf),
                pltpu.VMEM((keys, HEAD), f32),
                pltpu.VMEM((keys, HEAD), f32),
            ]
            + [pltpu.VMEM((slab, GROUP * BLOCK), t) for t in (f32, f32, bf, bf, bf, bf)],
        ),
        out_shape=out_shape,
        compiler_params=pltpu.CompilerParams(vmem_limit_bytes=VMEM_LIMIT),
        cost_estimate=MEDIUM if chunk else LIGHT,
        name="attention",
    )(place, opened, lo, *own, near, near, near, halo[0], halo[0], halo[1], halo[1], grad_out, near, *far_do)


def sum_kernel(heads, sc_ref, *refs):
    dk, dv = refs[-2:]
    core = sc_ref[0]
    for at in range(heads * 2):
        near, far = refs[2 * at : 2 * at + 2]
        half = core if at % 2 == 0 else 1 - core
        to = pl.ds(pl.multiple_of((half * heads + at // 2) * HEAD, HEAD), HEAD)
        total = near[...].astype(jnp.float32) + far[...].astype(jnp.float32)
        dk[:, to] = total[:, :HEAD].astype(dk.dtype)
        dv[:, to] = total[:, HEAD:].astype(dv.dtype)


def sum_terms(place, chunk, heads, n_heads, terms, before, after):
    pair = 2 * HEAD
    rows = terms[0][0].shape[0]
    hbm = pl.BlockSpec(memory_space=pl.ANY)

    def spec(x, by_core, column):
        return pl.BlockSpec((rows, pair), lambda g, sc: (sc[0] if by_core else 0, column))

    shape = jax.ShapeDtypeStruct((rows, n_heads * HEAD), jnp.bfloat16)
    return pl.pallas_call(
        functools.partial(sum_kernel, heads),
        grid_spec=pltpu.PrefetchScalarGridSpec(
            num_scalar_prefetch=1,
            grid=(1,),
            in_specs=[spec(*t) for t in terms] + [hbm] * len((*before, *after)),
            out_specs=[pl.BlockSpec((rows, 2 * heads * HEAD), lambda g, sc: (0, chunk))] * 2,
        ),
        out_shape=[shape, shape],
        input_output_aliases={len(terms) + 1: 0, len(terms) + 2: 1} if before else {},
        compiler_params=pltpu.CompilerParams(vmem_limit_bytes=VMEM_LIMIT),
        cost_estimate=LIGHT,
        name="sum_terms",
    )(place, *[t[0] for t in terms], *before, *after)


def body(queries, keys, values, grad_out, band_mask, segment_ids):
    n_ctx, n_mp = lax.axis_size("ctx"), lax.axis_size("mp")
    rows = queries.shape[0]
    piece = rows // n_mp
    heads_mp = KV_HEADS // n_mp
    heads = heads_mp // (2 * CHUNKS)
    pair = GROUP * HEAD
    wide = heads * pair
    bf = jnp.bfloat16
    ctx, mp = lax.axis_index("ctx"), lax.axis_index("mp")
    core, chip = lax.rem(ctx, 2), ctx // 2
    place = jnp.stack([core, mp]).astype(jnp.int32)

    def send(x, target):
        return lax.ppermute(x, AXES, routes(target, n_ctx, n_mp))

    swap = lambda c, m: (c ^ 1, m)

    def first_head(chunk, core):
        return (2 * chunk + core) * heads

    def col(head, width):
        return pl.multiple_of(head * width, HEAD)

    def plan_halo(chunk):
        def plan(core, mp):
            jobs, by = [], heads * HEAD
            for side in range(2):
                src = col(first_head(chunk, core if side == 0 else 1 - core), HEAD)
                for n in range(2):
                    dst, to = (side, n) if chunk == 0 else (0, 2 * side + n)
                    jobs.append((n, dst, (0, src), (0, to * by), (rows, by)))
            return jobs

        return plan

    def pack_halo(chunk, after):
        shapes = [(rows, wide)] * 2 if chunk == 0 else [(rows, 2 * wide)]
        return gather(plan_halo(chunk), 4, (keys, values), shapes, HEAVY, after, "pack_halo")

    far = [(dk, dm) for dm in range(1, n_mp) for dk in range(2)]
    n_far = n_mp - 1

    def plan_near(core, mp):
        jobs = []
        for dm in range(1, n_mp):
            mp_to = lax.rem(mp + dm, n_mp)
            for i in range(CHUNKS):
                for side in range(2):
                    core_to = core if side == 0 else 1 - core
                    src = col(mp_to * heads_mp + first_head(i, core_to), pair)
                    at = i * n_far + dm - 1
                    jobs.append((3, at, (0, src), (0, side * wide), (piece, wide)))
        for n, width, to in ((0, pair, 0), (1, HEAD, CHUNKS * wide), (2, HEAD, 3 * CHUNKS * wide // 2)):
            for i in range(CHUNKS):
                src = col(first_head(i, 1 - core), width)
                by = heads * width
                jobs.append((n, CHUNKS * n_far, (0, src), (0, to + i * by), (rows, by)))
        for i in range(CHUNKS):
            src = col(mp * heads_mp + first_head(i, 1 - core), pair)
            jobs.append((3, CHUNKS * n_far, (0, src), (i * piece, 2 * CHUNKS * wide), (piece, wide)))
        return jobs

    halos = [pack_halo(0, ())]
    *far_do, near = gather(
        plan_near,
        CHUNKS * (2 * n_far + 4),
        (queries, keys, values, grad_out),
        [(piece, 2 * wide)] * (CHUNKS * n_far) + [(rows, (2 * CHUNKS + 1) * wide)],
        HEAVY,
        halos[0],
        "pack_near",
    )
    far_do = [
        [
            send(far_do[i * n_far + dm - 1], lambda c, m: (c, (m + dm) % n_mp))
            for dm in range(1, n_mp)
        ]
        for i in range(CHUNKS)
    ]
    halos += [pack_halo(i, (near,)) for i in range(1, CHUNKS)]
    halo_in = [
        [send(x, lambda c, m: ((c + 2) ^ side, m)) for side, x in enumerate(halo)] for halo in halos
    ]
    near = send(near, swap)

    tokens = 2 * rows
    padded = jnp.concatenate([jnp.full((WINDOW,), -1, jnp.int32), segment_ids])
    ids = lax.dynamic_slice_in_dim(padded, chip * tokens, WINDOW + tokens, 0)
    before = jnp.sum((ids[:, None] < ids[None, WINDOW:]).astype(jnp.int32), axis=0)
    lo = jnp.maximum(before, jnp.arange(1, tokens + 1, dtype=jnp.int32))[None, :]
    blocks = tokens // BLOCK
    opened = lax.dynamic_slice_in_dim(band_mask, chip * blocks, blocks, 0).reshape(-1)

    out_parts, dq_parts, across_parts, near_parts, far_parts = [], [], [], [], []
    for i in range(CHUNKS):
        halo, ahead = halo_in[i], halos[i + 1 :]
        if i:
            halo, far_do[i], dq_parts = lax.optimization_barrier((halo, far_do[i], dq_parts))
        else:
            far_do[i], ahead, lo, opened = lax.optimization_barrier((far_do[i], ahead, lo, opened))
        halo = (halo[0], halo[1] if i == 0 else send(halo[0], swap))
        last = i == CHUNKS - 1
        dq_same, dkv_same, across, o_own, *o_far = attention(
            n_mp,
            rows,
            not last,
            i,
            heads,
            place,
            opened,
            lo,
            (queries, keys, values),
            near,
            halo,
            grad_out,
            [y for x in far_do[i] for y in (x, send(x, swap))],
        )
        n_far_o = 2 * n_mp - 1
        o_far, back = o_far[:n_far_o], o_far[n_far_o:]
        if i:
            earlier = (out_parts[-1], across_parts[-1])
            (back, o_far, across), earlier = lax.optimization_barrier(((back, o_far, across), earlier))
            out_parts[-1], across_parts[-1] = earlier
        if last:
            far_parts.append(
                [
                    send(back[0], lambda c, m: (c - 2, m)),
                    send(back[1], lambda c, m: ((c - 2) ^ 1 if c >= 2 else -1, m)),
                ]
            )
        else:
            far_parts.append([send(back[0], lambda c, m: (c - 2, m))])
        o_parts = [
            send(o_far[1 + at], lambda c, m: (c ^ dk, (m + dm) % n_mp))
            for at, (dk, dm) in enumerate(far)
        ]
        o_oth = o_far[0]
        if last:
            o_oth, far_parts[-2][0] = lax.optimization_barrier((o_oth, far_parts[-2][0]))
        out_parts.append([o_own, send(o_oth, swap), *o_parts])
        across_parts.append(send(across, swap))
        dq_parts.append(dq_same)
        near_parts.append(dkv_same)

    arrays = [
        x for o, a, q in zip(out_parts, across_parts, dq_parts) for x in (*o, a, q)
    ]

    def plan_out(core, mp):
        jobs, at = [], 0
        for i in range(CHUNKS):
            for dk, dm in [(0, 0), (1, 0)] + far:
                mp_from, core_from = lax.rem(mp + n_mp - dm, n_mp), core if dk == 0 else 1 - core
                to = col(mp_from * heads_mp + first_head(i, core_from), pair)
                jobs.append((at, 0, (0, 0), (0, to), (piece, wide)))
                at += 1
            to = col(first_head(i, 1 - core), pair)
            jobs.append((at, 1, (0, 0), (0, to), (rows, wide)))
            to = col(first_head(i, core), pair)
            jobs.append((at + 1, 1, (0, 0), (0, to), (rows, wide)))
            at += 2
        return jobs

    attn_out, grad_queries = gather(
        plan_out,
        CHUNKS * (len(far) + 4),
        arrays,
        [(piece, n_mp * heads_mp * pair), (rows, heads_mp * pair)],
        LIGHT,
        (),
        "put_together",
    )

    grads_kv = ()
    for i in range(CHUNKS):
        terms = []
        if i < CHUNKS - 1:
            back, far_parts[-1][0] = lax.optimization_barrier((far_parts[i][0], far_parts[-1][0]))
            handed = [
                send(lax.dynamic_slice(back, ((1 - core) * rows, g * pair), (rows, pair)), swap)
                for g in range(heads)
            ]
        for g in range(heads):
            last = i == CHUNKS - 1
            terms += [(near_parts[i], False, g), (far_parts[i][0], not last, g)]
            terms += [(across_parts[i], False, heads + g)]
            terms += [(far_parts[i][1], False, g) if last else (handed[g], False, 0)]
        grads_kv = sum_terms(place, i, heads, heads_mp, terms, grads_kv, (attn_out,))
    return attn_out, grad_queries, grads_kv[0], grads_kv[1]


def solution(mesh):
    placed = (P("ctx", "mp"), P("ctx", "mp"), P("ctx", "mp"), P(("ctx", "mp"), None), P(), P())
    return jax.shard_map(
        body,
        mesh=mesh,
        in_specs=placed,
        out_specs=(P(("ctx", "mp"), None), P("ctx", "mp"), P("ctx", "mp"), P("ctx", "mp")),
        check_vma=False,
    )
```

```python
import functools
import math

import jax
import jax.numpy as jnp
from jax import lax
from jax.experimental import pallas as pl
from jax.experimental.pallas import tpu as pltpu
from jax.sharding import PartitionSpec as P

KV_HEADS = 16
GROUP = 2
HEAD = 128
WINDOW = 1024
BLOCK = 128
SPAN = WINDOW // BLOCK + 1
CHUNKS = 2
ATTN_SCALE = 168.0 ** (-0.5)
EXP2_SCALE = ATTN_SCALE * math.log2(math.e)
MASKED = -1e30
FAR = 1 << 20
AXES = ("ctx", "mp")
NT = (((1,), (1,)), ((), ()))
NN = (((1,), (0,)), ((), ()))
LIGHT = pl.CostEstimate(flops=0, bytes_accessed=1024, transcendentals=0)
VMEM_LIMIT = (64 * 1024 - 128) * 1024
MEDIUM = pl.CostEstimate(flops=4_000_000_000, bytes_accessed=1024, transcendentals=0)
HEAVY = pl.CostEstimate(flops=25_000_000_000, bytes_accessed=1024, transcendentals=0)


def dot(a, b, dims=NN):
    return lax.dot_general(a, b, dims, preferred_element_type=jnp.float32)


def routes(target, n_ctx, n_mp):
    out = []
    for c in range(n_ctx):
        for m in range(n_mp):
            d = target(c, m)
            if 0 <= d[0] < n_ctx:
                out.append((c * n_mp + m, d[0] * n_mp + d[1]))
    return out


def gather_kernel(plan, n_in, shapes, *refs):
    n = len(shapes)
    outs, images, sems = refs[n_in : n_in + n], refs[n_in + n : n_in + 2 * n], refs[-2:]
    into = [[] for _ in shapes]
    count = 0
    for src, dst, src_at, dst_at, size in plan(lax.rem(lax.axis_index("ctx"), 2), lax.axis_index("mp")):
        copy = pltpu.make_async_copy(
            refs[src].at[tuple(pl.ds(at, by) for at, by in zip(src_at, size))],
            images[dst].at[tuple(pl.ds(at, by) for at, by in zip(dst_at, size))],
            sems[0].at[count],
        )
        copy.start()
        into[dst].append(copy)
        count += 1
    written = []
    for dst in range(n):
        for copy in into[dst]:
            copy.wait()
        written.append(pltpu.make_async_copy(images[dst], outs[dst], sems[1].at[dst]))
        written[-1].start()
    for copy in written:
        copy.wait()


def gather(plan, count, arrays, shapes, cost, after=(), name="gather"):
    hbm = pl.BlockSpec(memory_space=pl.ANY)
    return pl.pallas_call(
        functools.partial(gather_kernel, plan, len(arrays) + len(after), shapes),
        in_specs=[hbm] * (len(arrays) + len(after)),
        out_specs=[hbm] * len(shapes),
        out_shape=[jax.ShapeDtypeStruct(shape, jnp.bfloat16) for shape in shapes],
        scratch_shapes=[pltpu.VMEM(shape, jnp.bfloat16) for shape in shapes]
        + [pltpu.SemaphoreType.DMA((count,)), pltpu.SemaphoreType.DMA((len(shapes),))],
        compiler_params=pltpu.CompilerParams(vmem_limit_bytes=VMEM_LIMIT),
        cost_estimate=cost,
        name=name,
    )(*arrays, *after)


def attention_kernel(n_mp, rows, whole, sc_ref, open_ref, lo_ref, *refs):
    q_own, k_own, v_own, q_near, k_near, v_near = refs[:6]
    kh_same, vh_same, kh_oth, vh_oth, do_own, do_oth = refs[6:12]
    do_far = refs[12 : 10 + 2 * n_mp]
    refs = refs[10 + 2 * n_mp :]
    n_back = 1 if whole else 2
    dq_same, dkv_same, across, o_own, o_oth, *o_far = refs[: 3 + 2 * n_mp]
    back = refs[3 + 2 * n_mp : 3 + 2 * n_mp + n_back]
    refs = refs[3 + 2 * n_mp + n_back :]
    qs, ks, vs, k_t, v_t, dos, os, dqs, dk, dv = refs[:10]
    s_refs, e_refs, ds_refs = refs[-6:-4], refs[-4:-2], refs[-2:]
    core, mp = sc_ref[0], sc_ref[1]
    piece, pair = rows // n_mp, GROUP * HEAD
    same = pl.ds(pl.multiple_of(core * rows, rows), rows)
    oth = pl.ds(pl.multiple_of((1 - core) * rows, rows), rows)
    same_kv = pl.ds(pl.multiple_of(WINDOW + core * rows, rows), rows)
    oth_kv = pl.ds(pl.multiple_of(WINDOW + (1 - core) * rows, rows), rows)

    def piece_at(dk_, dm):
        k_at = core if dk_ == 0 else 1 - core
        return pl.ds(pl.multiple_of(k_at * rows + lax.rem(mp + dm, n_mp) * piece, piece), piece)

    qs[same, :] = q_own[...]
    qs[oth, :] = q_near[...]
    ks[same, :] = kh_same[...]
    ks[oth, :] = kh_oth[...]
    ks[same_kv, :] = k_own[...]
    ks[oth_kv, :] = k_near[...]
    vs[same, :] = vh_same[...]
    vs[oth, :] = vh_oth[...]
    vs[same_kv, :] = v_own[...]
    vs[oth_kv, :] = v_near[...]
    dos[piece_at(0, 0), :] = do_own[...]
    dos[piece_at(1, 0), :] = do_oth[...]
    for at in range(n_mp - 1):
        dos[piece_at(0, n_mp - 1 - at), :] = do_far[2 * at][...]
        dos[piece_at(1, n_mp - 1 - at), :] = do_far[2 * at + 1][...]
    for t in range(ks.shape[0] // 256):
        at = slice(t * 256, t * 256 + 256)
        k_t[:, at] = ks[at, :].T
        v_t[:, at] = vs[at, :].T

    width = GROUP * BLOCK
    row = lax.broadcasted_iota(jnp.int32, (BLOCK, width), 0)
    lane = lax.broadcasted_iota(jnp.int32, (BLOCK, width), 1)
    causal = row <= lax.rem(lane, BLOCK)

    def by_rows(x, reduce):
        return reduce(x.reshape(BLOCK // 8, 8, width), axis=0)

    def forward(b):
        s_ref, e_ref = s_refs[b % 2], e_refs[b % 2]
        at_q = slice(b * BLOCK, b * BLOCK + BLOCK)
        q_blk = jnp.concatenate([qs[at_q, :HEAD], qs[at_q, HEAD:]], axis=0)
        lo = jnp.concatenate([lo_ref[:, at_q]] * GROUP, axis=1)
        top = jnp.full((8, width), MASKED, jnp.float32)
        for j in range(SPAN):
            part = slice(j * BLOCK, j * BLOCK + BLOCK)
            s = dot(ks[(b + j) * BLOCK : (b + j + 1) * BLOCK, :], q_blk, NT)
            closed = jnp.where(open_ref[b * SPAN + SPAN - 1 - j] == 1, 0, FAR)
            valid = row >= jnp.maximum(lo - (b + j) * BLOCK, closed)
            if j == SPAN - 1:
                valid = valid & causal
            s = jnp.where(valid, s, MASKED)
            s_ref[part, :] = s
            top = jnp.maximum(top, by_rows(s, jnp.max))
        top = jnp.max(top, axis=0, keepdims=True)
        total = jnp.zeros((8, width), jnp.float32)
        for j in range(SPAN):
            part = slice(j * BLOCK, j * BLOCK + BLOCK)
            e = jnp.exp2((s_ref[part, :] - top) * EXP2_SCALE)
            total = total + by_rows(e, jnp.sum)
            e_ref[part, :] = e.astype(jnp.bfloat16)
        return q_blk, 1.0 / jnp.sum(total, axis=0, keepdims=True)

    def backward(b, q_blk, inverse):
        e_ref, ds_ref = e_refs[b % 2], ds_refs[b % 2]
        at_q = slice(b * BLOCK, b * BLOCK + BLOCK)
        at_keys = slice(b * BLOCK, (b + SPAN) * BLOCK)
        o_t = (dot(v_t[:, at_keys], e_ref[...]) * inverse).astype(jnp.bfloat16)
        os[at_q, :HEAD] = o_t[:, :BLOCK].T
        os[at_q, HEAD:] = o_t[:, BLOCK:].T
        do_t = jnp.concatenate([dos[at_q, :HEAD].T, dos[at_q, HEAD:].T], axis=1)
        do_t = (do_t.astype(jnp.float32) * inverse).astype(jnp.bfloat16)
        delta = jnp.sum(
            do_t.astype(jnp.float32) * o_t.astype(jnp.float32), axis=0, keepdims=True
        )
        for j in range(SPAN):
            part = slice(j * BLOCK, j * BLOCK + BLOCK)
            dp = dot(vs[(b + j) * BLOCK : (b + j + 1) * BLOCK, :], do_t)
            ds_ref[part, :] = (e_ref[part, :].astype(jnp.float32) * (dp - delta)).astype(
                jnp.bfloat16
            )
        for total, part in ((dv, dot(e_ref[...], do_t, NT)), (dk, dot(ds_ref[...], q_blk))):
            met = 0 if b == 0 else WINDOW
            seen, fresh = slice(b * BLOCK, b * BLOCK + met), slice(b * BLOCK + met, (b + SPAN) * BLOCK)
            if met:
                total[seen, :] += part[:met]
            total[fresh, :] = part[met:]
        dq_t = (dot(k_t[:, at_keys], ds_ref[...]) * ATTN_SCALE).astype(jnp.bfloat16)
        dqs[at_q, :HEAD] = dq_t[:, :BLOCK].T
        dqs[at_q, HEAD:] = dq_t[:, BLOCK:].T

    blocks = qs.shape[0] // BLOCK
    ahead = forward(0)
    for b in range(blocks):
        now, ahead = ahead, forward(b + 1) if b + 1 < blocks else None
        backward(b, *now)

    dq_same[...] = dqs[same, :]
    wide = across.shape[1] // 2
    at_g = pl.multiple_of(pl.program_id(0) * pair, pair)
    across[:, pl.ds(at_g, pair)] = dqs[oth, :]
    o_own[...] = os[piece_at(0, 0), :]
    o_oth[...] = os[piece_at(1, 0), :]
    for at in range(n_mp - 1):
        o_far[2 * at][...] = os[piece_at(0, at + 1), :]
        o_far[2 * at + 1][...] = os[piece_at(1, at + 1), :]
    back = (back[0].at[:rows], back[0].at[rows:]) if whole else back
    for out, at in ((dkv_same, same_kv), (back[0], same), (back[1], oth)):
        out[:, :HEAD] = (dk[at, :] * ATTN_SCALE).astype(out.dtype)
        out[:, HEAD:] = dv[at, :].astype(out.dtype)
    across[:, pl.ds(wide + at_g, HEAD)] = (dk[oth_kv, :] * ATTN_SCALE).astype(across.dtype)
    across[:, pl.ds(wide + at_g + HEAD, HEAD)] = dv[oth_kv, :].astype(across.dtype)


def attention(n_mp, rows, whole, chunk, heads, place, opened, lo, own, near, halo, grad_out, far_do):
    heads_mp = 2 * CHUNKS * heads
    piece, pair = rows // n_mp, GROUP * HEAD
    heads_chunk, first = heads, chunk * heads

    def at_head(g, sc, *unused):
        return (0, 2 * first + sc[0] * heads + g)

    def at_grad(g, sc, *unused):
        return (0, sc[1] * heads_mp + 2 * first + sc[0] * heads + g)

    def at_near(column):
        return lambda g, *unused: (0, column + first + g)

    def at_near_do(g, *unused):
        return (chunk, CHUNKS * 2 * heads + g)

    def at_halo(which, side):
        skip = 2 * heads if side and chunk else 0
        return lambda g, *unused: (0, skip + which * heads + g)

    def at_local(g, *unused):
        return (0, g)

    def at_handed(g, *unused):
        return (0, heads + g)

    in_specs = [pl.BlockSpec((1, 2 * rows), lambda g, *unused: (0, 0))]
    in_specs += [pl.BlockSpec((rows, pair), at_head)]
    in_specs += [pl.BlockSpec((rows, HEAD), at_head)] * 2
    in_specs += [pl.BlockSpec((rows, pair), at_near(0))]
    in_specs += [pl.BlockSpec((rows, HEAD), at_near(n * CHUNKS * heads)) for n in (2, 3)]
    in_specs += [pl.BlockSpec((rows, HEAD), at_halo(n % 2, n // 2)) for n in range(4)]
    in_specs += [pl.BlockSpec((piece, pair), at_grad), pl.BlockSpec((piece, pair), at_near_do)]
    in_specs += [pl.BlockSpec((piece, pair), at) for at in (at_local, at_handed)] * (n_mp - 1)
    wide = heads_chunk * pair
    bf, f32 = jnp.bfloat16, jnp.float32
    out_specs = [pl.BlockSpec((rows, pair), at_local)] * 2
    out_specs += [pl.BlockSpec((rows, 2 * wide), lambda g, *unused: (0, 0))]
    out_specs += [pl.BlockSpec((piece, pair), at_local)] * (2 * n_mp)
    out_shape = [jax.ShapeDtypeStruct((rows, wide), bf)] * 2
    out_shape += [jax.ShapeDtypeStruct((rows, 2 * wide), bf)]
    out_shape += [jax.ShapeDtypeStruct((piece, wide), bf)] * (2 * n_mp)
    n_back, rows_back = (1, 2 * rows) if whole else (2, rows)
    out_specs += [pl.BlockSpec((rows_back, pair), at_local)] * n_back
    out_shape += [jax.ShapeDtypeStruct((rows_back, wide), bf)] * n_back
    tokens, keys, slab = 2 * rows, WINDOW + 2 * rows, SPAN * BLOCK
    return pl.pallas_call(
        functools.partial(attention_kernel, n_mp, rows, whole),
        grid_spec=pltpu.PrefetchScalarGridSpec(
            num_scalar_prefetch=2,
            grid=(heads_chunk,),
            in_specs=in_specs,
            out_specs=out_specs,
            scratch_shapes=[
                pltpu.VMEM((tokens, pair), bf),
                pltpu.VMEM((keys, HEAD), bf),
                pltpu.VMEM((keys, HEAD), bf),
                pltpu.VMEM((HEAD, keys), bf),
                pltpu.VMEM((HEAD, keys), bf),
                pltpu.VMEM((tokens, pair), bf),
                pltpu.VMEM((tokens, pair), bf),
                pltpu.VMEM((tokens, pair), bf),
                pltpu.VMEM((keys, HEAD), f32),
                pltpu.VMEM((keys, HEAD), f32),
            ]
            + [pltpu.VMEM((slab, GROUP * BLOCK), t) for t in (f32, f32, bf, bf, bf, bf)],
        ),
        out_shape=out_shape,
        compiler_params=pltpu.CompilerParams(vmem_limit_bytes=VMEM_LIMIT),
        cost_estimate=MEDIUM if chunk else LIGHT,
        name="attention",
    )(place, opened, lo, *own, near, near, near, halo[0], halo[0], halo[1], halo[1], grad_out, near, *far_do)


def sum_kernel(heads, sc_ref, *refs):
    dk, dv = refs[-2:]
    core = sc_ref[0]
    for at in range(heads * 2):
        near, far = refs[2 * at : 2 * at + 2]
        half = core if at % 2 == 0 else 1 - core
        to = pl.ds(pl.multiple_of((half * heads + at // 2) * HEAD, HEAD), HEAD)
        total = near[...].astype(jnp.float32) + far[...].astype(jnp.float32)
        dk[:, to] = total[:, :HEAD].astype(dk.dtype)
        dv[:, to] = total[:, HEAD:].astype(dv.dtype)


def sum_terms(place, chunk, heads, n_heads, terms, before, after):
    pair = 2 * HEAD
    rows = terms[0][0].shape[0]
    hbm = pl.BlockSpec(memory_space=pl.ANY)

    def spec(x, by_core, column):
        return pl.BlockSpec((rows, pair), lambda g, sc: (sc[0] if by_core else 0, column))

    shape = jax.ShapeDtypeStruct((rows, n_heads * HEAD), jnp.bfloat16)
    return pl.pallas_call(
        functools.partial(sum_kernel, heads),
        grid_spec=pltpu.PrefetchScalarGridSpec(
            num_scalar_prefetch=1,
            grid=(1,),
            in_specs=[spec(*t) for t in terms] + [hbm] * len((*before, *after)),
            out_specs=[pl.BlockSpec((rows, 2 * heads * HEAD), lambda g, sc: (0, chunk))] * 2,
        ),
        out_shape=[shape, shape],
        input_output_aliases={len(terms) + 1: 0, len(terms) + 2: 1} if before else {},
        compiler_params=pltpu.CompilerParams(vmem_limit_bytes=VMEM_LIMIT),
        cost_estimate=LIGHT,
        name="sum_terms",
    )(place, *[t[0] for t in terms], *before, *after)


def body(queries, keys, values, grad_out, band_mask, segment_ids):
    n_ctx, n_mp = lax.axis_size("ctx"), lax.axis_size("mp")
    rows = queries.shape[0]
    piece = rows // n_mp
    heads_mp = KV_HEADS // n_mp
    heads = heads_mp // (2 * CHUNKS)
    pair = GROUP * HEAD
    wide = heads * pair
    bf = jnp.bfloat16
    ctx, mp = lax.axis_index("ctx"), lax.axis_index("mp")
    core, chip = lax.rem(ctx, 2), ctx // 2
    place = jnp.stack([core, mp]).astype(jnp.int32)

    def send(x, target):
        return lax.ppermute(x, AXES, routes(target, n_ctx, n_mp))

    swap = lambda c, m: (c ^ 1, m)

    def first_head(chunk, core):
        return (2 * chunk + core) * heads

    def col(head, width):
        return pl.multiple_of(head * width, HEAD)

    def plan_halo(chunk):
        def plan(core, mp):
            jobs, by = [], heads * HEAD
            for side in range(2):
                src = col(first_head(chunk, core if side == 0 else 1 - core), HEAD)
                for n in range(2):
                    dst, to = (side, n) if chunk == 0 else (0, 2 * side + n)
                    jobs.append((n, dst, (0, src), (0, to * by), (rows, by)))
            return jobs

        return plan

    def pack_halo(chunk, after):
        shapes = [(rows, wide)] * 2 if chunk == 0 else [(rows, 2 * wide)]
        return gather(plan_halo(chunk), 4, (keys, values), shapes, HEAVY, after, "pack_halo")

    far = [(dk, dm) for dm in range(1, n_mp) for dk in range(2)]
    n_far = n_mp - 1

    def plan_near(core, mp):
        jobs = []
        for dm in range(1, n_mp):
            mp_to = lax.rem(mp + dm, n_mp)
            for i in range(CHUNKS):
                for side in range(2):
                    core_to = core if side == 0 else 1 - core
                    src = col(mp_to * heads_mp + first_head(i, core_to), pair)
                    at = i * n_far + dm - 1
                    jobs.append((3, at, (0, src), (0, side * wide), (piece, wide)))
        for n, width, to in ((0, pair, 0), (1, HEAD, CHUNKS * wide), (2, HEAD, 3 * CHUNKS * wide // 2)):
            for i in range(CHUNKS):
                src = col(first_head(i, 1 - core), width)
                by = heads * width
                jobs.append((n, CHUNKS * n_far, (0, src), (0, to + i * by), (rows, by)))
        for i in range(CHUNKS):
            src = col(mp * heads_mp + first_head(i, 1 - core), pair)
            jobs.append((3, CHUNKS * n_far, (0, src), (i * piece, 2 * CHUNKS * wide), (piece, wide)))
        return jobs

    halos = [pack_halo(0, ())]
    *far_do, near = gather(
        plan_near,
        CHUNKS * (2 * n_far + 4),
        (queries, keys, values, grad_out),
        [(piece, 2 * wide)] * (CHUNKS * n_far) + [(rows, (2 * CHUNKS + 1) * wide)],
        HEAVY,
        halos[0],
        "pack_near",
    )
    far_do = [
        [
            send(far_do[i * n_far + dm - 1], lambda c, m: (c, (m + dm) % n_mp))
            for dm in range(1, n_mp)
        ]
        for i in range(CHUNKS)
    ]
    halos += [pack_halo(i, (near,)) for i in range(1, CHUNKS)]
    halo_in = [
        [send(x, lambda c, m: ((c + 2) ^ side, m)) for side, x in enumerate(halo)] for halo in halos
    ]
    near = send(near, swap)

    tokens = 2 * rows
    padded = jnp.concatenate([jnp.full((WINDOW,), -1, jnp.int32), segment_ids])
    ids = lax.dynamic_slice_in_dim(padded, chip * tokens, WINDOW + tokens, 0)
    before = jnp.sum((ids[:, None] < ids[None, WINDOW:]).astype(jnp.int32), axis=0)
    lo = jnp.maximum(before, jnp.arange(1, tokens + 1, dtype=jnp.int32))[None, :]
    blocks = tokens // BLOCK
    opened = lax.dynamic_slice_in_dim(band_mask, chip * blocks, blocks, 0).reshape(-1)

    out_parts, dq_parts, across_parts, near_parts, far_parts = [], [], [], [], []
    for i in range(CHUNKS):
        halo, ahead = halo_in[i], halos[i + 1 :]
        if i:
            halo, far_do[i], dq_parts = lax.optimization_barrier((halo, far_do[i], dq_parts))
        else:
            far_do[i], ahead, lo, opened = lax.optimization_barrier((far_do[i], ahead, lo, opened))
        halo = (halo[0], halo[1] if i == 0 else send(halo[0], swap))
        last = i == CHUNKS - 1
        dq_same, dkv_same, across, o_own, *o_far = attention(
            n_mp,
            rows,
            not last,
            i,
            heads,
            place,
            opened,
            lo,
            (queries, keys, values),
            near,
            halo,
            grad_out,
            [y for x in far_do[i] for y in (x, send(x, swap))],
        )
        n_far_o = 2 * n_mp - 1
        o_far, back = o_far[:n_far_o], o_far[n_far_o:]
        if i:
            earlier = (out_parts[-1], across_parts[-1])
            (back, o_far, across), earlier = lax.optimization_barrier(((back, o_far, across), earlier))
            out_parts[-1], across_parts[-1] = earlier
        if last:
            far_parts.append(
                [
                    send(back[0], lambda c, m: (c - 2, m)),
                    send(back[1], lambda c, m: ((c - 2) ^ 1 if c >= 2 else -1, m)),
                ]
            )
        else:
            far_parts.append([send(back[0], lambda c, m: (c - 2, m))])
        o_parts = [
            send(o_far[1 + at], lambda c, m: (c ^ dk, (m + dm) % n_mp))
            for at, (dk, dm) in enumerate(far)
        ]
        o_oth = o_far[0]
        if last:
            o_oth, far_parts[-2][0] = lax.optimization_barrier((o_oth, far_parts[-2][0]))
        out_parts.append([o_own, send(o_oth, swap), *o_parts])
        across_parts.append(send(across, swap))
        dq_parts.append(dq_same)
        near_parts.append(dkv_same)

    arrays = [
        x for o, a, q in zip(out_parts, across_parts, dq_parts) for x in (*o, a, q)
    ]

    def plan_out(core, mp):
        jobs, at = [], 0
        for i in range(CHUNKS):
            for dk, dm in [(0, 0), (1, 0)] + far:
                mp_from, core_from = lax.rem(mp + n_mp - dm, n_mp), core if dk == 0 else 1 - core
                to = col(mp_from * heads_mp + first_head(i, core_from), pair)
                jobs.append((at, 0, (0, 0), (0, to), (piece, wide)))
                at += 1
            to = col(first_head(i, 1 - core), pair)
            jobs.append((at, 1, (0, 0), (0, to), (rows, wide)))
            to = col(first_head(i, core), pair)
            jobs.append((at + 1, 1, (0, 0), (0, to), (rows, wide)))
            at += 2
        return jobs

    attn_out, grad_queries = gather(
        plan_out,
        CHUNKS * (len(far) + 4),
        arrays,
        [(piece, n_mp * heads_mp * pair), (rows, heads_mp * pair)],
        LIGHT,
        (),
        "put_together",
    )

    grads_kv = ()
    for i in range(CHUNKS):
        terms = []
        if i < CHUNKS - 1:
            back, far_parts[-1][0] = lax.optimization_barrier((far_parts[i][0], far_parts[-1][0]))
            handed = [
                send(back[rows:, g * pair : (g + 1) * pair], swap)
                for g in range(heads)
            ]
        for g in range(heads):
            last = i == CHUNKS - 1
            terms += [(near_parts[i], False, g), (far_parts[i][0], False, g)]
            terms += [(across_parts[i], False, heads + g)]
            terms += [(far_parts[i][1], False, g) if last else (handed[g], False, 0)]
        grads_kv = sum_terms(place, i, heads, heads_mp, terms, grads_kv, (attn_out,))
    return attn_out, grad_queries, grads_kv[0], grads_kv[1]


def solution(mesh):
    placed = (P("ctx", "mp"), P("ctx", "mp"), P("ctx", "mp"), P(("ctx", "mp"), None), P(), P())
    return jax.shard_map(
        body,
        mesh=mesh,
        in_specs=placed,
        out_specs=(P(("ctx", "mp"), None), P("ctx", "mp"), P("ctx", "mp"), P("ctx", "mp")),
        check_vma=False,
    )
```
